32 devices in a mesh: slab: 2 (over y), gy: 4 (over z), gx: 4 (over x, core).
Axes of the slice: x: 2, y: 2, z: 4, core: 2. Of those that a mesh axis runs over, the one named last changes fastest.
Arguments:
- volume: float32 [8, 256, 1024], P(None, ('slab', 'gy'), 'gx'), parts along dimension 1, may hold values from -8 to 8
- tissue_mask: int32 [2, 32, 128], P(None, ('slab', 'gy'), 'gx'), parts along dimension 1, may hold values from 0 to 1
- smoothing: float32 [1], replicated, may hold values from 0.7 to 1.4
Outputs:
- filtered: float32 [8, 256, 1024], P(None, ('slab', 'gy'), 'gx'), parts along dimension 1
The draws below stay inside these ranges and needn't reach their ends.
There are 2 independent parts, one for each index of `slab`. The reference program is written for one: setup_inputs(seed, part) draws one part's arguments, and reference() takes and returns one part's arrays. A program takes and returns all parts, laid end to end along the dimension named above; an argument that names none is the same for every part. Nothing has to cross between parts.
All inputs are finite; a program needn't handle non-finite values.
Results may differ from the reference program's by a relative error of at most 0.00002.
Values sent between devices are 32-bit elements; how exact they have to be, the bound alone decides.
No kernel may reach another device: no remote copies, remote signals or barrier semaphores. Data moves between devices by JAX's collectives and lax.ppermute only.
A program may use at most 64 MiB of HBM per device.

```python
import jax
import jax.numpy as jnp

Z = 8
ITERS = 2
NY = 128
NX = 1024


def draw_volume(key, part):
    first_key = jax.random.fold_in(key, 11)
    second_key = jax.random.fold_in(key, 12)
    rows_pos = jnp.arange(NY).astype(jnp.float32)
    row_scale = jnp.exp(jnp.log(3.0) * rows_pos / (NY - 1))[None, :, None]
    levels = 1.5 * jax.random.normal(second_key, (Z // 4, NY // 8, NX // 8), jnp.float32)
    spread = jnp.broadcast_to(levels[:, None, :, None, :, None], (Z // 4, 4, NY // 8, 8, NX // 8, 8)).reshape(Z, NY, NX)
    noise = jax.random.normal(first_key, (Z, NY, NX), jnp.float32)
    result = spread + noise * row_scale
    return jnp.clip(result, -8.0, 8.0)


def draw_tissue_mask(key, part):
    mask_key = jax.random.fold_in(key, 21)
    rolls = jax.random.randint(mask_key, (Z // 4, NY // 8, NX // 8), 0, 1000)
    rows_pos = jnp.arange(NY // 8)
    limits = 300 + 600 * rows_pos // max(NY // 8 - 1, 1)
    return (rolls < limits[None, :, None]).astype(jnp.int32)


def setup_inputs(seed: int = 0, part: int = 0) -> dict:
    seeds = jax.random.split(jax.random.key(seed), 4)
    part_splits = jax.random.split(jax.random.fold_in(seeds[3], part), 4)
    return {
        "volume": draw_volume(jax.random.fold_in(jax.random.fold_in(seeds[3], part), 71), part),
        "tissue_mask": draw_tissue_mask(jax.random.fold_in(jax.random.fold_in(seeds[3], part), 71), part),
        "smoothing": jnp.clip(jax.random.uniform(seeds[2], (1,), jnp.float32, 0.7, 1.4), 0.7, 1.4),
    }


OFFSETS = [(a, b, c) for a in (-4, 0, 4) for b in (-8, 0, 8) for c in (-8, 0, 8)]


def expand_mask(tissue_mask):
    blocks_z, blocks_y, blocks_x = tissue_mask.shape
    spread = jnp.broadcast_to(tissue_mask[:, None, :, None, :, None], (blocks_z, 4, blocks_y, 8, blocks_x, 8))
    return spread.reshape(blocks_z * 4, blocks_y * 8, blocks_x * 8).astype(jnp.float32)


def noise_terms(values, tissue):
    residual = values[1:-1] - 0.5 * (values[:-2] + values[2:])
    inner = tissue[1:-1]
    summed = jnp.sum(inner * residual * residual) * (2.0 / 3.0)
    return summed, jnp.sum(inner)


def box_sum(squared, depth, rows, cols):
    first = squared[0:depth] + squared[1:depth + 1] + squared[2:depth + 2]
    second = first[:, 0:rows] + first[:, 1:rows + 1] + first[:, 2:rows + 2]
    return second[:, :, 0:cols] + second[:, :, 1:cols + 1] + second[:, :, 2:cols + 2]


def smooth_once(padded_vals, padded_tiss, values, tissue, inverse_width):
    depth, rows, cols = values.shape
    centre = padded_vals[4:depth + 6, 8:rows + 10, 8:cols + 10]
    numerator = jnp.zeros(values.shape, jnp.float32)
    denominator = jnp.zeros(values.shape, jnp.float32)
    for offset in OFFSETS:
        shift_z, shift_y, shift_x = offset
        moved = padded_vals[4 + shift_z:depth + 6 + shift_z, 8 + shift_y:rows + 10 + shift_y, 8 + shift_x:cols + 10 + shift_x]
        differ = centre - moved
        distance = box_sum(differ * differ, depth, rows, cols)
        other_tiss = padded_tiss[5 + shift_z:5 + shift_z + depth, 9 + shift_y:9 + shift_y + rows, 9 + shift_x:9 + shift_x + cols]
        other_vals = padded_vals[5 + shift_z:5 + shift_z + depth, 9 + shift_y:9 + shift_y + rows, 9 + shift_x:9 + shift_x + cols]
        weight_field = jnp.exp(-distance * inverse_width) * other_tiss
        numerator = numerator + weight_field * other_vals
        denominator = denominator + weight_field
    return tissue * numerator / (denominator + 1.0 - tissue) + (1.0 - tissue) * values


def reference(volume, tissue_mask, smoothing):
    tissue = expand_mask(tissue_mask)
    summed, tissue_count = noise_terms(volume, tissue)
    variance = summed / jnp.maximum(tissue_count, 1.0) + 1e-5
    inverse_width = 1.0 / (54.0 * smoothing[0] * smoothing[0] * variance)
    widths = ((5, 5), (9, 9), (9, 9))
    padded_tiss = jnp.pad(tissue, widths)
    values = volume
    for iteration in range(ITERS):
        padded_vals = jnp.pad(values, widths)
        values = smooth_once(padded_vals, padded_tiss, values, tissue, inverse_width)
    return values
```

```python
import functools

import jax
import jax.numpy as jnp
from jax import lax
from jax.experimental import pallas as pl
from jax.experimental.pallas import tpu as pltpu
from jax.sharding import PartitionSpec as P

F32 = jnp.float32
HALO = 18
OUT = HALO // 2
VMEM = pltpu.VMEM


def iotas():
    return (
        lax.broadcasted_iota(jnp.int32, (8, 128), 0),
        lax.broadcasted_iota(jnp.int32, (8, 128), 1),
    )


def lane_roll(x, by):
    return pltpu.roll(x, by % 128, 1)


def depth_roll(x, by):
    return pltpu.roll(x, by % 8, 0)


def pack_kernel(vol_ref, mask_ref, own_ref, low_ref, high_ref, sums_ref, stage):
    cols = own_ref.shape[2]
    rows = own_ref.shape[0] - mask_ref.shape[1]
    blocks = mask_ref.shape[1]
    tiles = cols // 128
    sub, lane = iotas()
    wide = lax.broadcasted_iota(jnp.int32, (mask_ref.shape[2], cols), 1) // 8
    spread = (wide == lax.broadcasted_iota(jnp.int32, wide.shape, 0)).astype(F32)
    half = lax.broadcasted_iota(jnp.int32, (8, mask_ref.shape[2]), 0) < 4
    tissue = []
    for b in range(blocks):
        picked = jnp.where(half, mask_ref[0, b : b + 1, :], mask_ref[1, b : b + 1, :])
        t = jnp.dot(picked.astype(F32), spread, preferred_element_type=F32)
        own_ref[rows + b] = t
        tissue.append(t)
    total = jnp.zeros((8, 128), F32)
    count = jnp.zeros((8, 128), F32)
    for t in range(tiles):
        sl = slice(t * 128, (t + 1) * 128)
        stage[...] = vol_ref[:, sl]
        for b in range(blocks):
            part = jnp.zeros((8, 128), F32)
            for y in range(b * 8, b * 8 + 8):
                v = stage[pl.ds(y, 8, stride=rows), :]
                own_ref[y, :, sl] = v
                res = v - 0.5 * (depth_roll(v, 1) + depth_roll(v, -1))
                part = part + res * res
            total = total + part * tissue[b][:, sl]
            count = count + tissue[b][:, sl]
    inner = (sub >= 1) & (sub <= 6)
    total = jnp.where(inner, total * (2.0 / 3.0), 0.0)
    count = jnp.where(inner, count * 8.0, 0.0)
    sums_ref[0] = total
    sums_ref[1] = count
    packs = (rows + blocks) // 4
    group = lane // 32
    for k in range(packs):
        low = own_ref[4 * k, :, 0:128]
        high = lane_roll(own_ref[4 * k, :, cols - 128 : cols], 32)
        for g in range(1, 4):
            low = jnp.where(group == g, lane_roll(own_ref[4 * k + g, :, 0:128], 32 * g), low)
            high = jnp.where(
                group == g, lane_roll(own_ref[4 * k + g, :, cols - 128 : cols], 32 * (g + 1)), high
            )
        low_ref[k] = low
        high_ref[k] = high
    for ref in (low_ref, high_ref):
        ref[packs] = total
        ref[packs + 1] = count


def widen_kernel(own_ref, left_ref, right_ref, own_sum_ref, far_ref, wide_ref, top_ref, bottom_ref, sums_ref):
    cols = own_ref.shape[2]
    count = own_ref.shape[0]
    blocks = count // 9
    rows = count - blocks
    packs = count // 4
    _, lane = iotas()
    place = lax.axis_index("gx")
    has_left = (place > 0).astype(F32)
    has_right = (place < lax.axis_size("gx") - 1).astype(F32)
    for k in range(packs):
        left = left_ref[k] * has_left
        right = right_ref[k] * has_right
        for g in range(4):
            edge = jnp.where(lane < HALO, lane_roll(right, -32 * g), 0.0)
            edge = jnp.where(lane >= 128 - HALO, lane_roll(left, 32 * (3 - g)), edge)
            wide_ref[4 * k + g, :, cols:] = edge
    wide_ref[:, :, 0:cols] = own_ref[...]
    top_ref[0:HALO] = wide_ref[0:HALO]
    bottom_ref[0:HALO] = wide_ref[rows - HALO : rows]
    top_ref[HALO : HALO + 3] = wide_ref[rows : rows + 3]
    bottom_ref[HALO : HALO + 3] = wide_ref[count - 3 : count]
    for i in range(2):
        s = own_sum_ref[i] + left_ref[packs + i] + right_ref[packs + i] + far_ref[i]
        sums_ref[i] = s
        for ref in (top_ref, bottom_ref):
            ref[HALO + 3, :, i * 128 : (i + 1) * 128] = s
    for ref in (top_ref, bottom_ref):
        ref[HALO + 3, :, 256:] = jnp.zeros((8, ref.shape[2] - 256), F32)


FIELDS = [(0, 8), (1, -8), (1, 0), (1, 8), (2, 8), (2, 0), (3, -8), (3, 0), (3, 8)]


def smooth_kernel(
    wide_ref, above_ref, below_ref, sums_ref, far_ref, smoothing_ref, out_ref, val, tis, cor, wgt, pair, stage
):
    count = wide_ref.shape[0]
    blocks = count // 9
    rows = count - blocks
    cols = out_ref.shape[1]
    ring = wide_ref.shape[2]
    tiles = ring // 128
    full = rows + 2 * HALO
    sub, lane = iotas()
    tile = [slice(t * 128, (t + 1) * 128) for t in range(tiles)]

    place = lax.axis_index("gy")
    has_above = (place > 0).astype(F32)
    has_below = (place < lax.axis_size("gy") - 1).astype(F32)

    total = sums_ref[0] + above_ref[HALO + 3, :, 0:128] + below_ref[HALO + 3, :, 0:128] + far_ref[0]
    number = (
        sums_ref[1] + above_ref[HALO + 3, :, 128:256] + below_ref[HALO + 3, :, 128:256] + far_ref[1]
    )
    total = jnp.sum(jnp.sum(total, axis=1, keepdims=True), axis=0, keepdims=True)
    number = jnp.sum(jnp.sum(number, axis=1, keepdims=True), axis=0, keepdims=True)
    variance = total / jnp.maximum(number, 1.0) + 1e-05
    h = smoothing_ref[0]
    inverse = 1.0 / (54.0 * h * h * variance)
    factor = jnp.broadcast_to(inverse * (-1.4426950408889634), (8, 128))

    def shift8(x):
        moved = [lane_roll(v, -8) for v in x]
        return [jnp.where(lane < 120, moved[t], moved[(t + 1) % tiles]) for t in range(tiles)]

    def unshift8(x):
        moved = [lane_roll(v, 8) for v in x]
        return [jnp.where(lane < 8, moved[(t - 1) % tiles], moved[t]) for t in range(tiles)]

    def box_lanes(x):
        up = [lane_roll(v, 1) for v in x]
        down = [lane_roll(v, -1) for v in x]
        return [
            x[t]
            + jnp.where(lane == 0, up[(t - 1) % tiles], up[t])
            + jnp.where(lane == 127, down[(t + 1) % tiles], down[t])
            for t in range(tiles)
        ]

    def load(ref, *idx):
        return [ref[(*idx, slice(None), s)] for s in tile]

    def store(ref, x, *idx):
        for t, s in enumerate(tile):
            ref[(*idx, slice(None), s)] = x[t]

    val[0, HALO : HALO + rows] = wide_ref[0:rows]
    val[0, 0:HALO] = above_ref[0:HALO] * has_above
    val[0, HALO + rows : full] = below_ref[0:HALO] * has_below
    tis[0, 3 : 3 + blocks] = wide_ref[rows:count]
    tis[0, 0:3] = above_ref[HALO : HALO + 3] * has_above
    tis[0, 3 + blocks :] = below_ref[HALO : HALO + 3] * has_below
    spans = blocks + 6
    for b in range(spans):
        t0 = load(tis, 0, b)
        t1 = shift8(t0)
        store(tis, t1, 1, b)
        store(tis, [depth_roll(v, 4) for v in t0], 2, b)
        store(tis, [depth_roll(v, 4) for v in t1], 3, b)
    for f, (kind, step) in enumerate(FIELDS):
        for b in range(spans if step == 0 else spans - 1):
            low, high = b, b + (1 if step else 0)
            p, q = (high, low) if step < 0 else (low, high)
            for s in tile:
                pair[f, b, :, s] = tis[0, p, :, s] * tis[kind, q, :, s]

    edge34 = (sub == 3) | (sub == 4)
    edge04 = (sub == 0) | (sub == 4)
    edge37 = (sub == 3) | (sub == 7)

    def run_rows(start, number, group, fn):
        whole = number // group
        if whole:
            @pl.loop(0, whole)
            def _(i):
                fn(start + i * group, group)
        if number % group:
            fn(start + whole * group, number % group)

    def prepare(r, group):
        for i in range(group):
            v = load(val, 0, r + i)
            v8 = shift8(v)
            store(val, v8, 1, r + i)
            store(val, [depth_roll(x, 4) for x in v], 2, r + i)
            store(val, [depth_roll(x, 4) for x in v8], 3, r + i)

    def corrections(r, group):
        square = []
        for i in range(-1, group + 1):
            square.append([x * x for x in load(val, 0, r + i)])
        for i in range(group):
            s = [square[i][t] + square[i + 1][t] + square[i + 2][t] for t in range(tiles)]
            s = box_lanes(s)
            near = [jnp.where(sub == 3, depth_roll(x, -1), depth_roll(x, 1)) for x in s]
            far = [depth_roll(x, 4) for x in near]
            store(cor, near, 0, r + i)
            store(cor, far, 1, r + i)
            store(cor, shift8(far), 2, r + i)

    def weights(fields):
        def fn(r, group):
            for f in fields:
                kind, step = FIELDS[f]
                p = r + 8 if step < 0 else r
                q = r + 8 if step > 0 else r
                e = []
                for i in range(-1, group + 1):
                    d = [a - b for a, b in zip(load(val, 0, p + i), load(val, kind, q + i))]
                    e.append([x * x for x in d])
                for i in range(group):
                    s = [e[i][t] + e[i + 1][t] + e[i + 2][t] for t in range(tiles)]
                    s = box_lanes(s)
                    up = [depth_roll(x, 1) for x in s]
                    down = [depth_roll(x, -1) for x in s]
                    if kind >= 2:
                        c = [
                            jnp.where(edge34, a, b)
                            for a, b in zip(load(cor, 0, p + i), load(cor, kind - 1, q + i))
                        ]
                        up = [jnp.where(edge04, a, b) for a, b in zip(c, up)]
                        down = [jnp.where(edge37, a, b) for a, b in zip(c, down)]
                    else:
                        up = [jnp.where(sub == 0, 0.0, b) for b in up]
                        down = [jnp.where(sub == 7, 0.0, b) for b in down]
                    block = (r + i + 24 - HALO) // 8
                    both = load(pair, f, block)
                    w = [
                        jnp.exp2((s[t] + up[t] + down[t]) * factor) * both[t] for t in range(tiles)
                    ]
                    store(wgt, w, f, r + i)

        return fn

    def combine(last):
        def fn(r, group):
            for i in range(group):
                y = r + i
                centre = load(val, 0, y)
                own = load(tis, 0, (y + 24 - HALO) // 8)
                den = [None] * 4
                num = [None] * 4

                def add(frame, w, v):
                    if den[frame] is None:
                        den[frame] = list(w)
                        num[frame] = [a * b for a, b in zip(w, v)]
                    else:
                        den[frame] = [a + b for a, b in zip(den[frame], w)]
                        num[frame] = [n + a * b for n, a, b in zip(num[frame], w, v)]

                for f, (kind, step) in enumerate(FIELDS):
                    add(0, load(wgt, f, y - 8 if step < 0 else y), load(val, kind, y + step))
                    if (kind, step) != (2, 0):
                        add(kind, load(wgt, f, y - 8 if step > 0 else y), load(val, 0, y - step))
                result = []
                for acc in (den, num):
                    side = [a + depth_roll(b, 4) for a, b in zip(acc[1], acc[3])]
                    side = unshift8(side)
                    result.append(
                        [a + depth_roll(b, 4) + c for a, b, c in zip(acc[0], acc[2], side)]
                    )
                for t in range(cols // 128 if last else tiles):
                    d = result[0][t] + own[t] + (1.0 - own[t])
                    n = result[1][t] + own[t] * centre[t]
                    new = jnp.where(own[t] > 0.0, n / d, centre[t])
                    if last:
                        stage[t, pl.ds(y - HALO, 8, stride=rows), :] = new
                    else:
                        val[4, y, :, tile[t]] = new

        return fn

    apart = [f for f, (_, step) in enumerate(FIELDS) if step]
    level = [f for f, (_, step) in enumerate(FIELDS) if not step]
    for margin in (OUT, 2 * OUT):
        last = margin == 2 * OUT
        first, number = margin, full - 2 * margin
        run_rows(first - OUT, number + 2 * OUT, 2, prepare)
        run_rows(first - OUT + 1, number + 2 * OUT - 2, 2, corrections)
        for f in apart:
            run_rows(first - 8, number + 8, 4, weights([f]))
        for f in level:
            run_rows(first, number, 4, weights([f]))
        run_rows(first, number, 2, combine(last))
        if last:
            for t in range(cols // 128):
                out_ref[:, tile[t]] = stage[t]
        else:
            val[0, first : first + number] = val[4, first : first + number]


def on_device(volume, tissue_mask, smoothing):
    depth, rows, cols = volume.shape
    blocks = tissue_mask.shape[1]
    count = rows + blocks
    ring = cols + 128
    full = rows + 2 * HALO
    spans = blocks + 6
    vm = pl.BlockSpec(memory_space=VMEM)
    shape = lambda *s: jax.ShapeDtypeStruct(s, F32)
    params = pltpu.CompilerParams(vmem_limit_bytes=32 * 1024 * 1024)
    own, low, high, sums = pl.pallas_call(
        pack_kernel,
        out_shape=(
            shape(count, 8, cols),
            shape(count // 4 + 2, 8, 128),
            shape(count // 4 + 2, 8, 128),
            shape(2, 8, 128),
        ),
        in_specs=[vm, vm],
        out_specs=[vm] * 4,
        scratch_shapes=[pltpu.VMEM((depth * rows, 128), F32)],
        compiler_params=params,
        name="pack",
    )(volume.reshape(depth * rows, cols), tissue_mask)

    def send(x, axis, by):
        size = lax.axis_size(axis)
        return lax.ppermute(x, axis, [(i, (i + by) % size) for i in range(size)])

    def sums_beyond(x, axis):
        return functools.reduce(
            jnp.add, [send(x, axis, by) for by in range(2, lax.axis_size(axis) - 1)]
        )

    right = send(low, "gx", -1)
    left = send(high, "gx", 1)
    far = sums_beyond(sums, "gx")
    wide, top, bottom, sums = pl.pallas_call(
        widen_kernel,
        out_shape=(
            shape(count, 8, ring),
            shape(HALO + 4, 8, ring),
            shape(HALO + 4, 8, ring),
            shape(2, 8, 128),
        ),
        in_specs=[vm] * 5,
        out_specs=[vm] * 4,
        compiler_params=params,
        name="widen",
    )(own, left, right, sums, far)
    below = send(top, "gy", -1)
    above = send(bottom, "gy", 1)
    far = sums_beyond(sums, "gy")
    out = pl.pallas_call(
        smooth_kernel,
        out_shape=shape(depth * rows, cols),
        in_specs=[vm] * 5 + [pl.BlockSpec(memory_space=pltpu.SMEM)],
        out_specs=vm,
        scratch_shapes=[
            pltpu.VMEM((5, full, 8, ring), F32),
            pltpu.VMEM((4, spans, 8, ring), F32),
            pltpu.VMEM((3, full, 8, ring), F32),
            pltpu.VMEM((len(FIELDS), full, 8, ring), F32),
            pltpu.VMEM((len(FIELDS), spans, 8, ring), F32),
            pltpu.VMEM((cols // 128, depth * rows, 128), F32),
        ],
        compiler_params=params,
        name="smooth",
    )(wide, above, below, sums, far, smoothing)
    return out.reshape(depth, rows, cols)


def solution(mesh):
    placed = (P(None, ("slab", "gy"), "gx"), P(None, ("slab", "gy"), "gx"), P())
    return jax.shard_map(
        on_device,
        mesh=mesh,
        in_specs=placed,
        out_specs=P(None, ("slab", "gy"), "gx"),
        check_vma=False,
    )
```

```python
import functools

import jax
import jax.numpy as jnp
from jax import lax
from jax.experimental import pallas as pl
from jax.experimental.pallas import tpu as pltpu
from jax.sharding import PartitionSpec as P

F32 = jnp.float32
HALO = 18
OUT = HALO // 2
VMEM = pltpu.VMEM


def iotas():
    return (
        lax.broadcasted_iota(jnp.int32, (8, 128), 0),
        lax.broadcasted_iota(jnp.int32, (8, 128), 1),
    )


def lane_roll(x, by):
    return pltpu.roll(x, by % 128, 1)


def depth_roll(x, by):
    return pltpu.roll(x, by % 8, 0)


def permuted(x, source, count):
    lane = lax.broadcasted_iota(jnp.int32, (8, 128), 1)
    result = []
    for t in range(count):
        column = source(t, lane)
        index = lax.rem(column, 128)
        home = lax.div(column, 128)
        total = None
        for i, v in enumerate(x):
            part = jnp.take_along_axis(v, index, axis=1, mode="promise_in_bounds")
            total = part if total is None else jnp.where(home == i, part, total)
        result.append(total)
    return result


def pack_kernel(vol_ref, mask_ref, own_ref, low_ref, high_ref, sums_ref, stage):
    cols = own_ref.shape[2]
    rows = own_ref.shape[0] - mask_ref.shape[1]
    blocks = mask_ref.shape[1]
    tiles = cols // 128
    sub, lane = iotas()
    wide = lax.broadcasted_iota(jnp.int32, (mask_ref.shape[2], cols), 1) // 8
    spread = (wide == lax.broadcasted_iota(jnp.int32, wide.shape, 0)).astype(F32)
    half = lax.broadcasted_iota(jnp.int32, (8, mask_ref.shape[2]), 0) < 4
    tissue = []
    for b in range(blocks):
        picked = jnp.where(half, mask_ref[0, b : b + 1, :], mask_ref[1, b : b + 1, :])
        t = jnp.dot(picked.astype(F32), spread, preferred_element_type=F32)
        own_ref[rows + b] = t
        tissue.append(t)
    total = jnp.zeros((8, 128), F32)
    count = jnp.zeros((8, 128), F32)
    for t in range(tiles):
        sl = slice(t * 128, (t + 1) * 128)
        stage[...] = vol_ref[:, sl]
        for b in range(blocks):
            part = jnp.zeros((8, 128), F32)
            for y in range(b * 8, b * 8 + 8):
                v = stage[pl.ds(y, 8, stride=rows), :]
                own_ref[y, :, sl] = v
                res = v - 0.5 * (depth_roll(v, 1) + depth_roll(v, -1))
                part = part + res * res
            total = total + part * tissue[b][:, sl]
            count = count + tissue[b][:, sl]
    inner = (sub >= 1) & (sub <= 6)
    total = jnp.where(inner, total * (2.0 / 3.0), 0.0)
    count = jnp.where(inner, count * 8.0, 0.0)
    sums_ref[0] = total
    sums_ref[1] = count
    packs = (rows + blocks) // 4
    group = lane // 32
    for k in range(packs):
        low = own_ref[4 * k, :, 0:128]
        high = lane_roll(own_ref[4 * k, :, cols - 128 : cols], 32)
        for g in range(1, 4):
            low = jnp.where(group == g, lane_roll(own_ref[4 * k + g, :, 0:128], 32 * g), low)
            high = jnp.where(
                group == g, lane_roll(own_ref[4 * k + g, :, cols - 128 : cols], 32 * (g + 1)), high
            )
        low_ref[k] = low
        high_ref[k] = high
    for ref in (low_ref, high_ref):
        ref[packs] = total
        ref[packs + 1] = count


def widen_kernel(fars, own_ref, left_ref, right_ref, own_sum_ref, *refs):
    far_refs, (wide_ref, top_ref, bottom_ref, sums_ref) = refs[:fars], refs[fars:]
    cols = own_ref.shape[2]
    count = own_ref.shape[0]
    blocks = count // 9
    rows = count - blocks
    packs = count // 4
    tiles = cols // 128 + 1
    _, lane = iotas()
    place = lax.axis_index("gx")
    has_left = (place > 0).astype(F32)
    has_right = (place < lax.axis_size("gx") - 1).astype(F32)
    for k in range(packs):
        left = left_ref[k] * has_left
        right = right_ref[k] * has_right
        for g in range(4):
            edge = jnp.where(lane < HALO, lane_roll(right, -32 * g), 0.0)
            edge = jnp.where(lane >= 128 - HALO, lane_roll(left, 32 * (3 - g)), edge)
            row = [own_ref[4 * k + g, :, t * 128 : (t + 1) * 128] for t in range(tiles - 1)]
            row = permuted(row + [edge], lambda t, l: l * tiles + t, tiles)
            for t in range(tiles):
                wide_ref[4 * k + g, :, t * 128 : (t + 1) * 128] = row[t]
    top_ref[0:HALO] = wide_ref[0:HALO]
    bottom_ref[0:HALO] = wide_ref[rows - HALO : rows]
    top_ref[HALO : HALO + 3] = wide_ref[rows : rows + 3]
    bottom_ref[HALO : HALO + 3] = wide_ref[count - 3 : count]
    for i in range(2):
        s = own_sum_ref[i] + left_ref[packs + i] + right_ref[packs + i]
        for far_ref in far_refs:
            s = s + far_ref[i]
        sums_ref[i] = s
        for ref in (top_ref, bottom_ref):
            ref[HALO + 3, :, i * 128 : (i + 1) * 128] = s
    for ref in (top_ref, bottom_ref):
        ref[HALO + 3, :, 256:] = jnp.zeros((8, ref.shape[2] - 256), F32)


FIELDS = [(0, 8), (1, -8), (1, 0), (1, 8), (2, 8), (2, 0), (3, -8), (3, 0), (3, 8)]


def smooth_kernel(fars, wide_ref, above_ref, below_ref, sums_ref, smoothing_ref, *refs):
    far_refs, (out_ref, val, tis, cor, wgt, pair, stage) = refs[:fars], refs[fars:]
    count = wide_ref.shape[0]
    blocks = count // 9
    rows = count - blocks
    cols = out_ref.shape[1]
    ring = wide_ref.shape[2]
    tiles = ring // 128
    full = rows + 2 * HALO
    sub, lane = iotas()
    tile = [slice(t * 128, (t + 1) * 128) for t in range(tiles)]

    totals = [
        functools.reduce(jnp.add, [ref[i] for ref in (sums_ref, *far_refs)])
        + above_ref[HALO + 3, :, i * 128 : (i + 1) * 128]
        + below_ref[HALO + 3, :, i * 128 : (i + 1) * 128]
        for i in range(2)
    ]
    total, number = [
        jnp.sum(jnp.sum(x, axis=1, keepdims=True), axis=0, keepdims=True) for x in totals
    ]
    variance = total / jnp.maximum(number, 1.0) + 1e-05
    h = smoothing_ref[0]
    inverse = 1.0 / (54.0 * h * h * variance)
    factor = jnp.broadcast_to(inverse * (-1.4426950408889634), (8, 128))

    def along(x, by):
        moved = []
        for j in range(tiles):
            lanes, source = divmod(j + by, tiles)
            moved.append(lane_roll(x[source], -lanes) if lanes else x[source])
        return moved

    def box_lanes(x):
        down, up = along(x, -1), along(x, 1)
        return [x[t] + down[t] + up[t] for t in range(tiles)]

    def load(ref, *idx):
        return [ref[(*idx, slice(None), s)] for s in tile]

    def store(ref, x, *idx):
        for t, s in enumerate(tile):
            ref[(*idx, slice(None), s)] = x[t]

    val[0, HALO : HALO + rows] = wide_ref[0:rows]
    val[0, 0:HALO] = above_ref[0:HALO]
    val[0, HALO + rows : full] = below_ref[0:HALO]
    tis[0, 3 : 3 + blocks] = wide_ref[rows:count]
    tis[0, 0:3] = above_ref[HALO : HALO + 3]
    tis[0, 3 + blocks :] = below_ref[HALO : HALO + 3]
    spans = blocks + 6
    for b in range(spans):
        t0 = load(tis, 0, b)
        t1 = along(t0, 8)
        store(tis, t1, 1, b)
        store(tis, [depth_roll(v, 4) for v in t0], 2, b)
        store(tis, [depth_roll(v, 4) for v in t1], 3, b)
    for f, (kind, step) in enumerate(FIELDS):
        for b in range(spans if step == 0 else spans - 1):
            low, high = b, b + (1 if step else 0)
            p, q = (high, low) if step < 0 else (low, high)
            for s in tile:
                pair[f, b, :, s] = tis[0, p, :, s] * tis[kind, q, :, s]

    edge34 = (sub == 3) | (sub == 4)
    edge04 = (sub == 0) | (sub == 4)
    edge37 = (sub == 3) | (sub == 7)

    def run_rows(start, number, group, fn):
        whole = number // group
        if whole:
            @pl.loop(0, whole)
            def _(i):
                fn(start + i * group, group)
        if number % group:
            fn(start + whole * group, number % group)

    def prepare(r, group):
        for i in range(group):
            v = load(val, 0, r + i)
            v8 = along(v, 8)
            store(val, v8, 1, r + i)
            store(val, [depth_roll(x, 4) for x in v], 2, r + i)
            store(val, [depth_roll(x, 4) for x in v8], 3, r + i)

    def corrections(r, group):
        square = []
        for i in range(-1, group + 1):
            square.append([x * x for x in load(val, 0, r + i)])
        for i in range(group):
            s = [square[i][t] + square[i + 1][t] + square[i + 2][t] for t in range(tiles)]
            s = box_lanes(s)
            near = [jnp.where(sub == 3, depth_roll(x, -1), depth_roll(x, 1)) for x in s]
            far = [depth_roll(x, 4) for x in near]
            store(cor, near, 0, r + i)
            store(cor, far, 1, r + i)
            store(cor, along(far, 8), 2, r + i)

    def weights(fields):
        def fn(r, group):
            shared = {}
            for f in fields:
                kind, step = FIELDS[f]
                p = r + 8 if step < 0 else r
                q = r + 8 if step > 0 else r
                if (step < 0) not in shared:
                    shared[step < 0] = [load(val, 0, p + i) for i in range(-1, group + 1)]
                e = []
                for i in range(-1, group + 1):
                    d = [a - b for a, b in zip(shared[step < 0][i + 1], load(val, kind, q + i))]
                    e.append([x * x for x in d])
                for i in range(group):
                    s = [e[i][t] + e[i + 1][t] + e[i + 2][t] for t in range(tiles)]
                    s = box_lanes(s)
                    up = [depth_roll(x, 1) for x in s]
                    down = [depth_roll(x, -1) for x in s]
                    if kind >= 2:
                        c = [
                            jnp.where(edge34, a, b)
                            for a, b in zip(load(cor, 0, p + i), load(cor, kind - 1, q + i))
                        ]
                        up = [jnp.where(edge04, a, b) for a, b in zip(c, up)]
                        down = [jnp.where(edge37, a, b) for a, b in zip(c, down)]
                    else:
                        up = [jnp.where(sub == 0, 0.0, b) for b in up]
                        down = [jnp.where(sub == 7, 0.0, b) for b in down]
                    block = (r + i + 24 - HALO) // 8
                    both = load(pair, f, block)
                    w = [
                        jnp.exp2((s[t] + up[t] + down[t]) * factor) * both[t] for t in range(tiles)
                    ]
                    store(wgt, w, f, r + i)

        return fn

    def combine(last):
        def fn(r, group):
            for i in range(group):
                y = r + i
                centre = load(val, 0, y)
                own = load(tis, 0, (y + 24 - HALO) // 8)
                den = [None] * 4
                num = [None] * 4

                def add(frame, w, v):
                    if den[frame] is None:
                        den[frame] = list(w)
                        num[frame] = [a * b for a, b in zip(w, v)]
                    else:
                        den[frame] = [a + b for a, b in zip(den[frame], w)]
                        num[frame] = [n + a * b for n, a, b in zip(num[frame], w, v)]

                for f, (kind, step) in enumerate(FIELDS):
                    add(0, load(wgt, f, y - 8 if step < 0 else y), load(val, kind, y + step))
                    if (kind, step) != (2, 0):
                        add(kind, load(wgt, f, y - 8 if step > 0 else y), load(val, 0, y - step))
                result = []
                for acc in (den, num):
                    side = [a + depth_roll(b, 4) for a, b in zip(acc[1], acc[3])]
                    side = along(side, -8)
                    result.append(
                        [a + depth_roll(b, 4) + c for a, b, c in zip(acc[0], acc[2], side)]
                    )
                new = []
                for t in range(tiles):
                    d = result[0][t] + own[t] + (1.0 - own[t])
                    n = result[1][t] + own[t] * centre[t]
                    new.append(jnp.where(own[t] > 0.0, n / d, centre[t]))
                if last:
                    column = lambda t, l: l + 128 * t
                    where = lambda t, l: lax.rem(column(t, l), tiles) * 128 + lax.div(
                        column(t, l), tiles
                    )
                    for t, x in enumerate(permuted(new, where, cols // 128)):
                        stage[t, pl.ds(y - HALO, 8, stride=rows), :] = x
                else:
                    store(val, new, 4, y)

        return fn

    apart = [f for f, (_, step) in enumerate(FIELDS) if step]
    level = [f for f, (_, step) in enumerate(FIELDS) if not step]
    for margin in (OUT, 2 * OUT):
        last = margin == 2 * OUT
        first, number = margin, full - 2 * margin
        run_rows(first - OUT, number + 2 * OUT, 8, prepare)
        run_rows(first - OUT + 1, number + 2 * OUT - 2, 8, corrections)
        run_rows(first - 8, number + 8, 4, weights(apart))
        run_rows(first, number, 4, weights(level))
        run_rows(first, number, 4, combine(last))
        if last:
            for t in range(cols // 128):
                out_ref[:, tile[t]] = stage[t]
        else:
            val[0, first : first + number] = val[4, first : first + number]


def on_device(volume, tissue_mask, smoothing):
    depth, rows, cols = volume.shape
    blocks = tissue_mask.shape[1]
    count = rows + blocks
    lanes = cols + 128
    full = rows + 2 * HALO
    spans = blocks + 6
    vm = pl.BlockSpec(memory_space=VMEM)
    shape = lambda *s: jax.ShapeDtypeStruct(s, F32)
    params = pltpu.CompilerParams(vmem_limit_bytes=32 * 1024 * 1024)
    own, low, high, sums = pl.pallas_call(
        pack_kernel,
        out_shape=(
            shape(count, 8, cols),
            shape(count // 4 + 2, 8, 128),
            shape(count // 4 + 2, 8, 128),
            shape(2, 8, 128),
        ),
        in_specs=[vm, vm],
        out_specs=[vm] * 4,
        scratch_shapes=[pltpu.VMEM((depth * rows, 128), F32)],
        compiler_params=params,
        name="pack",
    )(volume.reshape(depth * rows, cols), tissue_mask)

    def ring(x, axis, by):
        size = lax.axis_size(axis)
        return lax.ppermute(x, axis, [(i, (i + by) % size) for i in range(size)])

    def line(x, axis, by):
        size = lax.axis_size(axis)
        return lax.ppermute(x, axis, [(i, i + by) for i in range(size) if 0 <= i + by < size])

    def beyond(x, axis):
        return [ring(x, axis, by) for by in range(2, lax.axis_size(axis) - 1)]

    def ends(x, axis):
        last = lax.axis_size(axis) - 1
        return [lax.ppermute(x, axis, [(0, last), (last, 0)])] if last > 1 else []

    right = ring(low, "gx", -1)
    left = ring(high, "gx", 1)
    far = beyond(sums, "gx")
    wide, top, bottom, sums = pl.pallas_call(
        functools.partial(widen_kernel, len(far)),
        out_shape=(
            shape(count, 8, lanes),
            shape(HALO + 4, 8, lanes),
            shape(HALO + 4, 8, lanes),
            shape(2, 8, 128),
        ),
        in_specs=[vm] * (4 + len(far)),
        out_specs=[vm] * 4,
        compiler_params=params,
        name="widen",
    )(own, left, right, sums, *far)
    below = line(top, "gy", -1)
    above = line(bottom, "gy", 1)
    far = beyond(sums, "gy") + ends(sums, "gy")
    out = pl.pallas_call(
        functools.partial(smooth_kernel, len(far)),
        out_shape=shape(depth * rows, cols),
        in_specs=[vm] * 4 + [pl.BlockSpec(memory_space=pltpu.SMEM)] + [vm] * len(far),
        out_specs=vm,
        scratch_shapes=[
            pltpu.VMEM((5, full, 8, lanes), F32),
            pltpu.VMEM((4, spans, 8, lanes), F32),
            pltpu.VMEM((3, full, 8, lanes), F32),
            pltpu.VMEM((len(FIELDS), full, 8, lanes), F32),
            pltpu.VMEM((len(FIELDS), spans, 8, lanes), F32),
            pltpu.VMEM((cols // 128, depth * rows, 128), F32),
        ],
        compiler_params=params,
        name="smooth",
    )(wide, above, below, sums, smoothing, *far)
    return out.reshape(depth, rows, cols)


def solution(mesh):
    placed = (P(None, ("slab", "gy"), "gx"), P(None, ("slab", "gy"), "gx"), P())
    return jax.shard_map(
        on_device,
        mesh=mesh,
        in_specs=placed,
        out_specs=P(None, ("slab", "gy"), "gx"),
        check_vma=False,
    )
```

```python
import functools

import jax
import jax.numpy as jnp
from jax import lax
from jax.experimental import pallas as pl
from jax.experimental.pallas import tpu as pltpu
from jax.sharding import PartitionSpec as P

F32 = jnp.float32
HALO = 18
OUT = HALO // 2
VMEM = pltpu.VMEM


def iotas():
    return (
        lax.broadcasted_iota(jnp.int32, (8, 128), 0),
        lax.broadcasted_iota(jnp.int32, (8, 128), 1),
    )


def lane_roll(x, by):
    return pltpu.roll(x, by % 128, 1)


def depth_roll(x, by):
    return pltpu.roll(x, by % 8, 0)


def permuted(x, source, count):
    lane = lax.broadcasted_iota(jnp.int32, (8, 128), 1)
    result = []
    for t in range(count):
        column = source(t, lane)
        index = lax.rem(column, 128)
        home = lax.div(column, 128)
        total = None
        for i, v in enumerate(x):
            part = jnp.take_along_axis(v, index, axis=1, mode="promise_in_bounds")
            total = part if total is None else jnp.where(home == i, part, total)
        result.append(total)
    return result


def pack_kernel(vol_ref, mask_ref, own_ref, low_ref, high_ref, sums_ref, stage):
    cols = own_ref.shape[2]
    rows = own_ref.shape[0] - mask_ref.shape[1]
    blocks = mask_ref.shape[1]
    tiles = cols // 128
    sub, lane = iotas()
    wide = lax.broadcasted_iota(jnp.int32, (mask_ref.shape[2], cols), 1) // 8
    spread = (wide == lax.broadcasted_iota(jnp.int32, wide.shape, 0)).astype(F32)
    half = lax.broadcasted_iota(jnp.int32, (8, mask_ref.shape[2]), 0) < 4
    tissue = []
    for b in range(blocks):
        picked = jnp.where(half, mask_ref[0, b : b + 1, :], mask_ref[1, b : b + 1, :])
        t = jnp.dot(picked.astype(F32), spread, preferred_element_type=F32)
        own_ref[rows + b] = t
        tissue.append(t)
    total = jnp.zeros((8, 128), F32)
    count = jnp.zeros((8, 128), F32)
    for t in range(tiles):
        sl = slice(t * 128, (t + 1) * 128)
        stage[...] = vol_ref[:, sl]
        for b in range(blocks):
            part = jnp.zeros((8, 128), F32)
            for y in range(b * 8, b * 8 + 8):
                v = stage[pl.ds(y, 8, stride=rows), :]
                own_ref[y, :, sl] = v
                res = v - 0.5 * (depth_roll(v, 1) + depth_roll(v, -1))
                part = part + res * res
            total = total + part * tissue[b][:, sl]
            count = count + tissue[b][:, sl]
    inner = (sub >= 1) & (sub <= 6)
    total = jnp.where(inner, total * (2.0 / 3.0), 0.0)
    count = jnp.where(inner, count * 8.0, 0.0)
    sums_ref[0] = total
    sums_ref[1] = count
    packs = (rows + blocks) // 4
    group = lane // 32
    for k in range(packs):
        low = own_ref[4 * k, :, 0:128]
        high = lane_roll(own_ref[4 * k, :, cols - 128 : cols], 32)
        for g in range(1, 4):
            low = jnp.where(group == g, lane_roll(own_ref[4 * k + g, :, 0:128], 32 * g), low)
            high = jnp.where(
                group == g, lane_roll(own_ref[4 * k + g, :, cols - 128 : cols], 32 * (g + 1)), high
            )
        low_ref[k] = low
        high_ref[k] = high
    for ref in (low_ref, high_ref):
        ref[packs] = total
        ref[packs + 1] = count


def sums_kernel(left_ref, right_ref, *refs):
    packs = left_ref.shape[0] - 2
    ends_ref, all_ref = refs[-1], refs[-2]
    place, last = lax.axis_index("gy"), lax.axis_size("gy") - 1
    at_end = ((place == 0) | (place == last)).astype(F32)
    for i in range(2):
        s = left_ref[packs + i] + right_ref[packs + i]
        for ref in refs[:-2]:
            s = s + ref[i]
        all_ref[i] = s
        ends_ref[i] = s * jnp.where(lax.axis_index("gx") % 2 == 0, 1.0, at_end)


def widen_kernel(own_ref, left_ref, right_ref, sums_ref, wide_ref, top_ref, bottom_ref):
    cols = own_ref.shape[2]
    count = own_ref.shape[0]
    blocks = count // 9
    rows = count - blocks
    packs = count // 4
    tiles = cols // 128 + 1
    _, lane = iotas()
    place = lax.axis_index("gx")
    has_left = (place > 0).astype(F32)
    has_right = (place < lax.axis_size("gx") - 1).astype(F32)
    for k in range(packs):
        left = left_ref[k] * has_left
        right = right_ref[k] * has_right
        for g in range(4):
            edge = jnp.where(lane < HALO, lane_roll(right, -32 * g), 0.0)
            edge = jnp.where(lane >= 128 - HALO, lane_roll(left, 32 * (3 - g)), edge)
            row = [own_ref[4 * k + g, :, t * 128 : (t + 1) * 128] for t in range(tiles - 1)]
            row = permuted(row + [edge], lambda t, l: l * tiles + t, tiles)
            for t in range(tiles):
                wide_ref[4 * k + g, :, t * 128 : (t + 1) * 128] = row[t]
    top_ref[0:HALO] = wide_ref[0:HALO]
    bottom_ref[0:HALO] = wide_ref[rows - HALO : rows]
    top_ref[HALO : HALO + 3] = wide_ref[rows : rows + 3]
    bottom_ref[HALO : HALO + 3] = wide_ref[count - 3 : count]
    for i in range(2):
        for ref in (top_ref, bottom_ref):
            ref[HALO + 3, :, i * 128 : (i + 1) * 128] = sums_ref[i]
    for ref in (top_ref, bottom_ref):
        ref[HALO + 3, :, 256:] = jnp.zeros((8, ref.shape[2] - 256), F32)


FIELDS = [(0, 8), (1, -8), (1, 0), (1, 8), (2, 8), (2, 0), (3, -8), (3, 0), (3, 8)]
APART = [f for f, (_, step) in enumerate(FIELDS) if step]
LEVEL = [f for f, (_, step) in enumerate(FIELDS) if not step]


class Steps:
    def __init__(self, val, cor, dist, tis, pair):
        self.val, self.cor, self.dist, self.tis, self.pair = val, cor, dist, tis, pair
        self.tiles = val.shape[-1] // 128
        self.tile = [slice(t * 128, (t + 1) * 128) for t in range(self.tiles)]
        self.sub, self.lane = iotas()
        self.edge34 = (self.sub == 3) | (self.sub == 4)
        self.edge04 = (self.sub == 0) | (self.sub == 4)
        self.edge37 = (self.sub == 3) | (self.sub == 7)

    def load(self, ref, *idx):
        return [ref[(*idx, slice(None), s)] for s in self.tile]

    def store(self, ref, x, *idx):
        for t, s in enumerate(self.tile):
            ref[(*idx, slice(None), s)] = x[t]

    def along(self, x, by):
        moved = []
        for j in range(self.tiles):
            lanes, source = divmod(j + by, self.tiles)
            moved.append(lane_roll(x[source], -lanes) if lanes else x[source])
        return moved

    def box_lanes(self, x):
        down, up = self.along(x, -1), self.along(x, 1)
        first = x[0] + up[0]
        second = first + up[1]
        return [first + down[0], second] + [
            (x[t] + down[t]) + up[t] for t in range(2, self.tiles)
        ]

    def box_rows(self, e):
        result = []
        for i in range(0, len(e) - 2, 2):
            middle = [a + b for a, b in zip(e[i + 1], e[i + 2])]
            result.append([a + b for a, b in zip(e[i], middle)])
            if i + 3 < len(e):
                result.append([a + b for a, b in zip(middle, e[i + 3])])
        return result

    def run(self, starts, number, group, fn):
        whole = number // group
        if whole:
            @pl.loop(0, whole)
            def _(i):
                for start in starts:
                    fn(start + i * group, group)
        if number % group:
            for start in starts:
                fn(start + whole * group, number % group)

    def tissue(self, spans):
        for b in spans:
            t0 = self.load(self.tis, 0, b)
            t1 = self.along(t0, 8)
            self.store(self.tis, t1, 1, b)
            self.store(self.tis, [depth_roll(v, 4) for v in t0], 2, b)
            self.store(self.tis, [depth_roll(v, 4) for v in t1], 3, b)

    def pairs(self, spans, level_spans):
        for f, (kind, step) in enumerate(FIELDS):
            for b in spans if step else level_spans:
                low, high = b, b + (1 if step else 0)
                p, q = (high, low) if step < 0 else (low, high)
                for s in self.tile:
                    self.pair[f, b, :, s] = self.tis[0, p, :, s] * self.tis[kind, q, :, s]

    def prepare(self, source):
        def fn(r, group):
            for i in range(group):
                v = self.load(self.val, source, r + i)
                v8 = self.along(v, 8)
                if source:
                    self.store(self.val, v, 0, r + i)
                self.store(self.val, v8, 1, r + i)
                self.store(self.val, [depth_roll(x, 4) for x in v], 2, r + i)
                self.store(self.val, [depth_roll(x, 4) for x in v8], 3, r + i)

        return fn

    def corrections(self, r, group):
        square = []
        for i in range(-1, group + 1):
            square.append([x * x for x in self.load(self.val, 0, r + i)])
        sums = self.box_rows(square)
        for base in range(0, group, 4):
            some = sums[base : base + 4]
            packed = [depth_roll(x, 4) for x in some[0]]
            for i, row in enumerate(some):
                for place, by in ((2 * i, 2 * i - 4), (2 * i + 1, 2 * i - 2)):
                    if place:
                        here = self.sub == place
                        packed = [
                            jnp.where(here, depth_roll(x, by), y) for x, y in zip(row, packed)
                        ]
            packed = self.box_lanes(packed)
            moved = self.along(packed, 8)
            for i in range(len(some)):
                y = r + base + i
                self.store(self.cor, [depth_roll(x, 3 - 2 * i) for x in packed], 0, y)
                self.store(self.cor, [depth_roll(x, 7 - 2 * i) for x in packed], 1, y)
                self.store(self.cor, [depth_roll(x, 7 - 2 * i) for x in moved], 2, y)

    def distances(self, fields):
        def fn(r, group):
            shared = {}
            for f in fields:
                kind, step = FIELDS[f]
                p = r + 8 if step < 0 else r
                q = r + 8 if step > 0 else r
                if (step < 0) not in shared:
                    shared[step < 0] = [
                        self.load(self.val, 0, p + i) for i in range(-1, group + 1)
                    ]
                e = []
                for i in range(-1, group + 1):
                    other = self.load(self.val, kind, q + i)
                    d = [a - b for a, b in zip(shared[step < 0][i + 1], other)]
                    e.append([x * x for x in d])
                for i, s in enumerate(self.box_rows(e)):
                    s = self.box_lanes(s)
                    up = [depth_roll(x, 1) for x in s]
                    down = [depth_roll(x, -1) for x in s]
                    if kind >= 2:
                        near = self.load(self.cor, 0, p + i)
                        far = self.load(self.cor, kind - 1, q + i)
                        c = [jnp.where(self.edge34, a, b) for a, b in zip(near, far)]
                        up = [jnp.where(self.edge04, a, b) for a, b in zip(c, up)]
                        down = [jnp.where(self.edge37, a, b) for a, b in zip(c, down)]
                    else:
                        up = [jnp.where(self.sub == 0, 0.0, b) for b in up]
                        down = [jnp.where(self.sub == 7, 0.0, b) for b in down]
                    self.store(
                        self.dist, [a + b + c for a, b, c in zip(s, up, down)], f, r + i
                    )

        return fn

    def weight(self, f, r, factor):
        both = self.load(self.pair, f, (r + 24 - HALO) // 8)
        d = self.load(self.dist, f, r)
        return [jnp.exp2(a * factor) * b for a, b in zip(d, both)]

    def early(self, factor):
        def fn(r, group):
            for i in range(group):
                for f in APART:
                    self.store(self.dist, self.weight(f, r + i, factor), f, r + i)

        return fn

    def combine(self, factor, put):
        def fn(r, group):
            for i in range(group):
                y = r + i
                centre = self.load(self.val, 0, y)
                own = self.load(self.tis, 0, (y + 24 - HALO) // 8)
                den = [None] * 4
                num = [None] * 4

                def add(frame, w, v):
                    if den[frame] is None:
                        den[frame] = list(w)
                        num[frame] = [a * b for a, b in zip(w, v)]
                    else:
                        den[frame] = [a + b for a, b in zip(den[frame], w)]
                        num[frame] = [n + a * b for n, a, b in zip(num[frame], w, v)]

                for f, (kind, step) in enumerate(FIELDS):
                    w = self.weight(f, y, factor)
                    before = w
                    if step:
                        before = self.load(self.dist, f, y - 8)
                        self.store(self.dist, w, f, y)
                    at_p, at_q = (before, w) if step < 0 else (w, before)
                    add(0, at_p, self.load(self.val, kind, y + step))
                    if (kind, step) != (2, 0):
                        add(kind, at_q, self.load(self.val, 0, y - step))
                result = []
                for acc in (den, num):
                    side = [a + depth_roll(b, 4) for a, b in zip(acc[1], acc[3])]
                    side = self.along(side, -8)
                    result.append(
                        [a + depth_roll(b, 4) + c for a, b, c in zip(acc[0], acc[2], side)]
                    )
                new = []
                for t in range(self.tiles):
                    d = result[0][t] + own[t] + (1.0 - own[t])
                    n = result[1][t] + own[t] * centre[t]
                    new.append(jnp.where(own[t] > 0.0, n / d, centre[t]))
                put(y, new)

        return fn


def inner_kernel(wide_ref, val, cor, dist, tis, pair):
    count = wide_ref.shape[0]
    blocks = count // 9
    rows = count - blocks
    low, high = HALO, HALO + rows
    steps = Steps(val, cor, dist, tis, pair)
    val[0, low:high] = wide_ref[0:rows]
    tis[0, 3 : 3 + blocks] = wide_ref[rows:count]
    steps.tissue(range(3, 3 + blocks))
    steps.pairs(range(3, 2 + blocks), range(3, 3 + blocks))
    steps.run([low], rows, 8, steps.prepare(0))
    steps.run([low + 1], rows - 2, 8, steps.corrections)
    steps.run([low + 1], rows - 10, 8, steps.distances(APART))
    steps.run([low + 1], rows - 2, 8, steps.distances(LEVEL))


def outer_kernel(above_ref, below_ref, sums_ref, *refs):
    part_ref, val, cor, dist, tis, pair = refs[5:]
    full = val.shape[1]
    rows = full - 2 * HALO
    spans = tis.shape[1]
    low, high = HALO, HALO + rows
    steps = Steps(val, cor, dist, tis, pair)

    val[0, 0:low] = above_ref[0:HALO]
    val[0, high:full] = below_ref[0:HALO]
    tis[0, 0:3] = above_ref[HALO : HALO + 3]
    tis[0, spans - 3 :] = below_ref[HALO : HALO + 3]
    ends = [*range(0, 3), *range(spans - 3, spans)]
    steps.tissue(ends)
    steps.pairs([*range(0, 3), *range(spans - 4, spans - 1)], ends)
    for i in range(2):
        lanes = slice(i * 128, (i + 1) * 128)
        part_ref[i] = sums_ref[i] + above_ref[HALO + 3, :, lanes] + below_ref[HALO + 3, :, lanes]

    steps.run([0, high], HALO, 6, steps.prepare(0))
    steps.run([1, high - 1], HALO, 6, steps.corrections)
    steps.run([OUT - 8, high - 9], low + 1 - (OUT - 8), 6, steps.distances(APART))
    steps.run([OUT, high - 1], low + 1 - OUT, 5, steps.distances(LEVEL))


def smooth_kernel(fars, part_ref, smoothing_ref, *refs):
    far_refs, refs = refs[:fars], refs[fars + 5 :]
    out_ref, val, cor, dist, tis, pair, stage = refs
    cols = out_ref.shape[1]
    full = val.shape[1]
    rows = full - 2 * HALO
    low = HALO
    steps = Steps(val, cor, dist, tis, pair)

    total, number = [
        jnp.sum(
            jnp.sum(
                functools.reduce(jnp.add, [ref[i] for ref in (part_ref, *far_refs)]),
                axis=1,
                keepdims=True,
            ),
            axis=0,
            keepdims=True,
        )
        for i in range(2)
    ]
    variance = total / jnp.maximum(number, 1.0) + 1e-05
    h = smoothing_ref[0]
    inverse = 1.0 / (54.0 * h * h * variance)
    factor = jnp.broadcast_to(inverse * (-1.4426950408889634), (8, 128))

    def keep(y, new):
        steps.store(val, new, 4, y)

    def finish(y, new):
        column = lambda t, l: l + 128 * t
        where = lambda t, l: lax.rem(column(t, l), steps.tiles) * 128 + lax.div(
            column(t, l), steps.tiles
        )
        for t, x in enumerate(permuted(new, where, cols // 128)):
            stage[t, pl.ds(y - HALO, 8, stride=rows), :] = x

    steps.run([OUT - 8], 8, 2, steps.early(factor))
    steps.run([OUT], full - 2 * OUT, 2, steps.combine(factor, keep))

    steps.run([OUT], full - 2 * OUT, 10, steps.prepare(4))
    steps.run([OUT + 1], full - 2 * OUT - 2, 8, steps.corrections)
    steps.run([low - 8], rows + 8, 8, steps.distances(APART))
    steps.run([low], rows, 8, steps.distances(LEVEL))
    steps.run([low - 8], 8, 2, steps.early(factor))
    steps.run([low], rows, 4, steps.combine(factor, finish))
    for t in range(cols // 128):
        out_ref[:, t * 128 : (t + 1) * 128] = stage[t]


def on_device(volume, tissue_mask, smoothing):
    depth, rows, cols = volume.shape
    blocks = tissue_mask.shape[1]
    count = rows + blocks
    lanes = cols + 128
    full = rows + 2 * HALO
    spans = blocks + 6
    vm = pl.BlockSpec(memory_space=VMEM)
    shape = lambda *s: jax.ShapeDtypeStruct(s, F32)
    params = pltpu.CompilerParams(vmem_limit_bytes=32 * 1024 * 1024)
    own, low, high, sums = pl.pallas_call(
        pack_kernel,
        out_shape=(
            shape(count, 8, cols),
            shape(count // 4 + 2, 8, 128),
            shape(count // 4 + 2, 8, 128),
            shape(2, 8, 128),
        ),
        in_specs=[vm, vm],
        out_specs=[vm] * 4,
        scratch_shapes=[pltpu.VMEM((depth * rows, 128), F32)],
        compiler_params=params,
        name="pack",
    )(volume.reshape(depth * rows, cols), tissue_mask)

    def ring(x, axis, by):
        size = lax.axis_size(axis)
        return lax.ppermute(x, axis, [(i, (i + by) % size) for i in range(size)])

    def line(x, axis, by):
        size = lax.axis_size(axis)
        return lax.ppermute(x, axis, [(i, i + by) for i in range(size) if 0 <= i + by < size])

    def beyond(x, axis):
        return [ring(x, axis, by) for by in range(2, lax.axis_size(axis) - 1)]

    def far_rows(x, ends):
        ny, nx = lax.axis_size("gy"), lax.axis_size("gx")
        shifts = list(range(2, ny - 1)) + [None]
        got = []
        for even, odd in zip(shifts[0::2], shifts[1::2]):
            pairs = []
            for y in range(ny):
                for c in range(nx):
                    by = odd if c % 2 else even
                    to = ny - 1 - y if by is None else (y + by) % ny
                    pairs.append((y * nx + c, to * nx + c))
            got.append(lax.ppermute(ends if odd is None else x, ("gy", "gx"), pairs))
        return functools.reduce(jnp.add, got)

    right = ring(low, "gx", -1)
    left = ring(high, "gx", 1)
    far = beyond(sums, "gx")
    sums, ends = pl.pallas_call(
        sums_kernel,
        out_shape=[shape(2, 8, 128)] * 2,
        in_specs=[vm] * (3 + len(far)),
        out_specs=[vm] * 2,
        compiler_params=params,
        name="sums",
    )(left, right, sums, *far)
    wide, top, bottom = pl.pallas_call(
        widen_kernel,
        out_shape=(
            shape(count, 8, lanes),
            shape(HALO + 4, 8, lanes),
            shape(HALO + 4, 8, lanes),
        ),
        in_specs=[vm] * 4,
        out_specs=[vm] * 3,
        compiler_params=params,
        name="widen",
    )(own, left, right, sums)
    below = line(top, "gy", -1)
    above = line(bottom, "gy", 1)
    state = [
        shape(5, full, 8, lanes),
        shape(3, full, 8, lanes),
        shape(len(FIELDS), full, 8, lanes),
        shape(4, spans, 8, lanes),
        shape(len(FIELDS), spans, 8, lanes),
    ]
    held = pl.pallas_call(
        inner_kernel,
        out_shape=state,
        in_specs=[vm],
        out_specs=[vm] * 5,
        compiler_params=params,
        cost_estimate=pl.CostEstimate(flops=20_000_000, bytes_accessed=8_000_000, transcendentals=0),
        name="inner",
    )(wide)
    sums, ends, *held = lax.optimization_barrier((sums, ends, *held))
    far = far_rows(sums, ends)
    part, *held = pl.pallas_call(
        outer_kernel,
        out_shape=[shape(2, 8, 128)] + state,
        in_specs=[vm] * 8,
        out_specs=[vm] * 6,
        input_output_aliases={3 + i: 1 + i for i in range(5)},
        compiler_params=params,
        cost_estimate=pl.CostEstimate(flops=20_000_000, bytes_accessed=8_000_000, transcendentals=0),
        name="outer",
    )(above, below, sums, *held)
    part, far = lax.optimization_barrier((part, far))
    far = [far, lax.ppermute(far, "gx", [(c, c ^ 1) for c in range(lax.axis_size("gx"))])]
    out = pl.pallas_call(
        functools.partial(smooth_kernel, len(far)),
        out_shape=[shape(depth * rows, cols)] + state,
        in_specs=[vm] + [pl.BlockSpec(memory_space=pltpu.SMEM)] + [vm] * (len(far) + 5),
        out_specs=[vm] * 6,
        input_output_aliases={2 + len(far) + i: 1 + i for i in range(5)},
        scratch_shapes=[pltpu.VMEM((cols // 128, depth * rows, 128), F32)],
        compiler_params=params,
        name="smooth",
    )(part, smoothing, *far, *held)[0]
    return out.reshape(depth, rows, cols)


def solution(mesh):
    placed = (P(None, ("slab", "gy"), "gx"), P(None, ("slab", "gy"), "gx"), P())
    return jax.shard_map(
        on_device,
        mesh=mesh,
        in_specs=placed,
        out_specs=P(None, ("slab", "gy"), "gx"),
        check_vma=False,
    )
```

```python
import functools

import jax
import jax.numpy as jnp
from jax import lax
from jax.experimental import pallas as pl
from jax.experimental.pallas import tpu as pltpu
from jax.sharding import PartitionSpec as P

F32 = jnp.float32
HALO = 18
OUT = HALO // 2
VMEM = pltpu.VMEM


def iotas():
    return (
        lax.broadcasted_iota(jnp.int32, (8, 128), 0),
        lax.broadcasted_iota(jnp.int32, (8, 128), 1),
    )


def lane_roll(x, by):
    return pltpu.roll(x, by % 128, 1)


def depth_roll(x, by):
    return pltpu.roll(x, by % 8, 0)


def picked(x, index):
    return jnp.take_along_axis(x, index, axis=1, mode="promise_in_bounds")


class Ring:
    def __init__(self, tiles):
        self.tiles = tiles
        lane = iotas()[1]
        self.lane = lane
        column = [lane * tiles + t for t in range(tiles)]
        self.index = [lax.rem(c, 128) for c in column]
        self.home = [lax.div(c, 128) for c in column]

    def own(self, x):
        result = []
        for index, home in zip(self.index, self.home):
            total = picked(x[0], index)
            for i in range(1, len(x)):
                total = jnp.where(home == i, picked(x[i], index), total)
            result.append(total)
        return result

    def edges(self, x, edge):
        last = self.tiles - 1
        return [
            jnp.where(home == last, picked(edge, index), v)
            for v, index, home in zip(x, self.index, self.home)
        ]

    def unpacked(self, left, right, group):
        edge = jnp.where(self.lane < HALO, lane_roll(right, -32 * group), 0.0)
        return jnp.where(self.lane >= 128 - HALO, lane_roll(left, 32 * (3 - group)), edge)

    def plain(self, x, count):
        result = []
        for t in range(count):
            column = self.lane + 128 * t
            index, home = lax.div(column, self.tiles), lax.rem(column, self.tiles)
            total = picked(x[0], index)
            for i in range(1, self.tiles):
                total = jnp.where(home == i, picked(x[i], index), total)
            result.append(total)
        return result


def split(ref, row, tiles):
    return [ref[row, :, t * 128 : (t + 1) * 128] for t in range(tiles)]


def put(ref, row, x):
    for t, v in enumerate(x):
        ref[row, :, t * 128 : (t + 1) * 128] = v


def pack_kernel(vol_ref, mask_ref, own_ref, low_ref, high_ref, sums_ref, stage):
    cols = own_ref.shape[2]
    rows = own_ref.shape[0] - mask_ref.shape[1]
    blocks = mask_ref.shape[1]
    tiles = cols // 128
    sub, lane = iotas()
    wide = lax.broadcasted_iota(jnp.int32, (mask_ref.shape[2], cols), 1) // 8
    spread = (wide == lax.broadcasted_iota(jnp.int32, wide.shape, 0)).astype(F32)
    half = lax.broadcasted_iota(jnp.int32, (8, mask_ref.shape[2]), 0) < 4
    tissue = []
    for b in range(blocks):
        picked = jnp.where(half, mask_ref[0, b : b + 1, :], mask_ref[1, b : b + 1, :])
        t = jnp.dot(picked.astype(F32), spread, preferred_element_type=F32)
        own_ref[rows + b] = t
        tissue.append(t)
    total = jnp.zeros((8, 128), F32)
    count = jnp.zeros((8, 128), F32)
    for t in range(tiles):
        sl = slice(t * 128, (t + 1) * 128)
        stage[...] = vol_ref[:, sl]
        for b in range(blocks):
            part = jnp.zeros((8, 128), F32)
            for y in range(b * 8, b * 8 + 8):
                v = stage[pl.ds(y, 8, stride=rows), :]
                own_ref[y, :, sl] = v
                res = v - 0.5 * (depth_roll(v, 1) + depth_roll(v, -1))
                part = part + res * res
            total = total + part * tissue[b][:, sl]
            count = count + tissue[b][:, sl]
    inner = (sub >= 1) & (sub <= 6)
    total = jnp.where(inner, total * (2.0 / 3.0), 0.0)
    count = jnp.where(inner, count * 8.0, 0.0)
    sums_ref[0] = total
    sums_ref[1] = count
    packs = (rows + blocks) // 4
    group = lane // 32
    for k in range(packs):
        low = own_ref[4 * k, :, 0:128]
        high = lane_roll(own_ref[4 * k, :, cols - 128 : cols], 32)
        for g in range(1, 4):
            low = jnp.where(group == g, lane_roll(own_ref[4 * k + g, :, 0:128], 32 * g), low)
            high = jnp.where(
                group == g, lane_roll(own_ref[4 * k + g, :, cols - 128 : cols], 32 * (g + 1)), high
            )
        low_ref[k] = low
        high_ref[k] = high
    for ref in (low_ref, high_ref):
        ref[packs] = total
        ref[packs + 1] = count


def half_kernel(left_ref, right_ref, own_ref, *refs):
    packs = left_ref.shape[0] - 2
    odd = lax.rem(lax.axis_index("gx"), 2).astype(F32)
    for i in range(2):
        left, right = left_ref[packs + i], right_ref[packs + i]
        if len(refs) == 1:
            refs[-1][i] = own_ref[i] + left * (1.0 - odd) + right * odd
        else:
            refs[-1][i] = 0.5 * functools.reduce(
                jnp.add, [ref[i] for ref in refs[:-1]], own_ref[i] + left + right
            )


def whole_kernel(half_ref, other_ref, sums_ref, ends_ref):
    place, last = lax.axis_index("gy"), lax.axis_size("gy") - 1
    at_end = ((place == 0) | (place == last)).astype(F32)
    for i in range(2):
        sums_ref[i] = half_ref[i] + other_ref[i]
        ends_ref[i] = sums_ref[i] * jnp.where(lax.rem(lax.axis_index("gx"), 2) == 0, 1.0, at_end)


def order_kernel(own_ref, wide_ref):
    tiles = own_ref.shape[2] // 128
    ring = Ring(tiles + 1)
    for i in range(own_ref.shape[0]):
        put(wide_ref, i, ring.own(split(own_ref, i, tiles)))


def widen_kernel(part_ref, left_ref, right_ref, half_ref, wide_ref, top_ref, bottom_ref):
    tiles = wide_ref.shape[2] // 128
    count = wide_ref.shape[0]
    rows = count - count // 9
    ring = Ring(tiles)
    place = lax.axis_index("gx")
    has_left = (place > 0).astype(F32)
    has_right = (place < lax.axis_size("gx") - 1).astype(F32)
    for k in range(count // 4):
        left = left_ref[k] * has_left
        right = right_ref[k] * has_right
        for g in range(4):
            i = 4 * k + g
            put(wide_ref, i, ring.edges(split(part_ref, i, tiles), ring.unpacked(left, right, g)))
    sub = iotas()[0]
    for ref, row, block in ((top_ref, 0, rows), (bottom_ref, rows - HALO, count - 3)):
        ref[0:HALO] = wide_ref[row : row + HALO]
        packed = [jnp.zeros((8, 128), F32)] * tiles
        for b in range(3):
            for i in range(2):
                some = [v[4 * i : 4 * i + 1] for v in split(wide_ref, block + b, tiles)]
                packed = [jnp.where(sub == 2 * b + i, x, y) for x, y in zip(some, packed)]
        put(ref, HALO, packed)
        put(ref, HALO + 1, [half_ref[0], half_ref[1]] + [packed[0]] * (tiles - 2))


FIELDS = [(0, 8), (1, -8), (1, 0), (1, 8), (2, 8), (2, 0), (3, -8), (3, 0), (3, 8)]
APART = [f for f, (_, step) in enumerate(FIELDS) if step]
LEVEL = [f for f, (_, step) in enumerate(FIELDS) if not step]


class Steps:
    def __init__(self, val, cor, dist, tis, pair):
        self.val, self.cor, self.dist, self.tis, self.pair = val, cor, dist, tis, pair
        self.tiles = val.shape[-1] // 128
        self.tile = [slice(t * 128, (t + 1) * 128) for t in range(self.tiles)]
        self.sub, self.lane = iotas()
        self.edge34 = (self.sub == 3) | (self.sub == 4)
        self.edge04 = (self.sub == 0) | (self.sub == 4)
        self.edge37 = (self.sub == 3) | (self.sub == 7)

    def load(self, ref, *idx):
        return [ref[(*idx, slice(None), s)] for s in self.tile]

    def store(self, ref, x, *idx):
        for t, s in enumerate(self.tile):
            ref[(*idx, slice(None), s)] = x[t]

    def along(self, x, by):
        moved = []
        for j in range(self.tiles):
            lanes, source = divmod(j + by, self.tiles)
            moved.append(lane_roll(x[source], -lanes) if lanes else x[source])
        return moved

    def box_lanes(self, x):
        down, up = self.along(x, -1), self.along(x, 1)
        first = x[0] + up[0]
        second = first + up[1]
        return [first + down[0], second] + [
            (x[t] + down[t]) + up[t] for t in range(2, self.tiles)
        ]

    def box_rows(self, e):
        result = []
        for i in range(0, len(e) - 2, 2):
            middle = [a + b for a, b in zip(e[i + 1], e[i + 2])]
            result.append([a + b for a, b in zip(e[i], middle)])
            if i + 3 < len(e):
                result.append([a + b for a, b in zip(middle, e[i + 3])])
        return result

    def run(self, starts, number, group, fn):
        whole = number // group
        if whole:
            @pl.loop(0, whole)
            def _(i):
                for start in starts:
                    fn(start + i * group, group)
        if number % group:
            for start in starts:
                fn(start + whole * group, number % group)

    def tissue(self, spans):
        for b in spans:
            t0 = self.load(self.tis, 0, b)
            t1 = self.along(t0, 8)
            self.store(self.tis, t1, 1, b)
            self.store(self.tis, [depth_roll(v, 4) for v in t0], 2, b)
            self.store(self.tis, [depth_roll(v, 4) for v in t1], 3, b)

    def pairs(self, spans, level_spans):
        for f, (kind, step) in enumerate(FIELDS):
            for b in spans if step else level_spans:
                low, high = b, b + (1 if step else 0)
                p, q = (high, low) if step < 0 else (low, high)
                for s in self.tile:
                    self.pair[f, b, :, s] = self.tis[0, p, :, s] * self.tis[kind, q, :, s]

    def prepare(self, source):
        def fn(r, group):
            for i in range(group):
                v = self.load(self.val, source, r + i)
                v8 = self.along(v, 8)
                if source:
                    self.store(self.val, v, 0, r + i)
                self.store(self.val, v8, 1, r + i)
                self.store(self.val, [depth_roll(x, 4) for x in v], 2, r + i)
                self.store(self.val, [depth_roll(x, 4) for x in v8], 3, r + i)

        return fn

    def corrections(self, r, group):
        square = []
        for i in range(-1, group + 1):
            square.append([x * x for x in self.load(self.val, 0, r + i)])
        sums = self.box_rows(square)
        for base in range(0, group, 4):
            some = sums[base : base + 4]
            packed = [depth_roll(x, 4) for x in some[0]]
            for i, row in enumerate(some):
                for place, by in ((2 * i, 2 * i - 4), (2 * i + 1, 2 * i - 2)):
                    if place:
                        here = self.sub == place
                        packed = [
                            jnp.where(here, depth_roll(x, by), y) for x, y in zip(row, packed)
                        ]
            packed = self.box_lanes(packed)
            moved = self.along(packed, 8)
            for i in range(len(some)):
                y = r + base + i
                self.store(self.cor, [depth_roll(x, 3 - 2 * i) for x in packed], 0, y)
                self.store(self.cor, [depth_roll(x, 7 - 2 * i) for x in packed], 1, y)
                self.store(self.cor, [depth_roll(x, 7 - 2 * i) for x in moved], 2, y)

    def distances(self, fields):
        def fn(r, group):
            shared = {}
            for f in fields:
                kind, step = FIELDS[f]
                p = r + 8 if step < 0 else r
                q = r + 8 if step > 0 else r
                if (step < 0) not in shared:
                    shared[step < 0] = [
                        self.load(self.val, 0, p + i) for i in range(-1, group + 1)
                    ]
                e = []
                for i in range(-1, group + 1):
                    other = self.load(self.val, kind, q + i)
                    d = [a - b for a, b in zip(shared[step < 0][i + 1], other)]
                    e.append([x * x for x in d])
                for i, s in enumerate(self.box_rows(e)):
                    s = self.box_lanes(s)
                    up = [depth_roll(x, 1) for x in s]
                    down = [depth_roll(x, -1) for x in s]
                    if kind >= 2:
                        near = self.load(self.cor, 0, p + i)
                        far = self.load(self.cor, kind - 1, q + i)
                        c = [jnp.where(self.edge34, a, b) for a, b in zip(near, far)]
                        up = [jnp.where(self.edge04, a, b) for a, b in zip(c, up)]
                        down = [jnp.where(self.edge37, a, b) for a, b in zip(c, down)]
                    else:
                        up = [jnp.where(self.sub == 0, 0.0, b) for b in up]
                        down = [jnp.where(self.sub == 7, 0.0, b) for b in down]
                    self.store(
                        self.dist, [a + b + c for a, b, c in zip(s, up, down)], f, r + i
                    )

        return fn

    def weight(self, f, r, factor):
        both = self.load(self.pair, f, (r + 24 - HALO) // 8)
        d = self.load(self.dist, f, r)
        return [jnp.exp2(a * factor) * b for a, b in zip(d, both)]

    def early(self, factor):
        def fn(r, group):
            for i in range(group):
                for f in APART:
                    self.store(self.dist, self.weight(f, r + i, factor), f, r + i)

        return fn

    def combine(self, factor, put):
        def fn(r, group):
            for i in range(group):
                y = r + i
                centre = self.load(self.val, 0, y)
                own = self.load(self.tis, 0, (y + 24 - HALO) // 8)
                den = [None] * 4
                num = [None] * 4

                def add(frame, w, v):
                    if den[frame] is None:
                        den[frame] = list(w)
                        num[frame] = [a * b for a, b in zip(w, v)]
                    else:
                        den[frame] = [a + b for a, b in zip(den[frame], w)]
                        num[frame] = [n + a * b for n, a, b in zip(num[frame], w, v)]

                for f, (kind, step) in enumerate(FIELDS):
                    w = self.weight(f, y, factor)
                    before = w
                    if step:
                        before = self.load(self.dist, f, y - 8)
                        self.store(self.dist, w, f, y)
                    at_p, at_q = (before, w) if step < 0 else (w, before)
                    add(0, at_p, self.load(self.val, kind, y + step))
                    if (kind, step) != (2, 0):
                        add(kind, at_q, self.load(self.val, 0, y - step))
                result = []
                for acc in (den, num):
                    side = [a + depth_roll(b, 4) for a, b in zip(acc[1], acc[3])]
                    side = self.along(side, -8)
                    result.append(
                        [a + depth_roll(b, 4) + c for a, b, c in zip(acc[0], acc[2], side)]
                    )
                new = []
                for t in range(self.tiles):
                    n, d = result[1][t] + centre[t], result[0][t] + 1.0
                    new.append(jnp.where(own[t] > 0.0, n / d, centre[t]))
                put(y, new)

        return fn


def inner_kernel(wide_ref, val, cor, dist, tis, pair):
    count = wide_ref.shape[0]
    blocks = count // 9
    rows = count - blocks
    low, high = HALO, HALO + rows
    steps = Steps(val, cor, dist, tis, pair)
    val[0, low:high] = wide_ref[0:rows]
    tis[0, 3 : 3 + blocks] = wide_ref[rows:count]
    steps.tissue(range(3, 3 + blocks))
    steps.pairs(range(3, 2 + blocks), range(3, 3 + blocks))
    steps.run([low], rows, 8, steps.prepare(0))
    steps.run([low + 1], rows - 2, 8, steps.corrections)
    steps.run([low + 1], rows - 10, 8, steps.distances(APART))
    steps.run([low + 1], rows - 2, 8, steps.distances(LEVEL))


def outer_kernel(above_ref, below_ref, *refs):
    part_ref, val, cor, dist, tis, pair = refs[5:]
    full = val.shape[1]
    rows = full - 2 * HALO
    spans = tis.shape[1]
    low, high = HALO, HALO + rows
    steps = Steps(val, cor, dist, tis, pair)

    for ref, row, block in ((above_ref, 0, 0), (below_ref, high, spans - 3)):
        val[0, row : row + HALO] = ref[0:HALO]
        packed = split(ref, HALO, steps.tiles)
        for b in range(3):
            steps.store(
                tis,
                [
                    jnp.where(steps.sub < 4, v[2 * b : 2 * b + 1], v[2 * b + 1 : 2 * b + 2])
                    for v in packed
                ],
                0,
                block + b,
            )
    ends = [*range(0, 3), *range(spans - 3, spans)]
    steps.tissue(ends)
    steps.pairs([*range(0, 3), *range(spans - 4, spans - 1)], ends)
    for i in range(2):
        lanes = slice(i * 128, (i + 1) * 128)
        part_ref[i] = above_ref[HALO + 1, :, lanes] + below_ref[HALO + 1, :, lanes]

    steps.run([0, high], HALO, 6, steps.prepare(0))
    steps.run([1, high - 1], HALO, 6, steps.corrections)
    steps.run([OUT - 8, high - 9], low + 1 - (OUT - 8), 6, steps.distances(APART))
    steps.run([OUT, high - 1], low + 1 - OUT, 5, steps.distances(LEVEL))


def smooth_kernel(fars, sums_ref, smoothing_ref, *refs):
    far_refs, refs = refs[:fars], refs[fars + 5 :]
    out_ref, val, cor, dist, tis, pair, stage = refs
    cols = out_ref.shape[1]
    full = val.shape[1]
    rows = full - 2 * HALO
    low = HALO
    steps = Steps(val, cor, dist, tis, pair)
    ring = Ring(steps.tiles)

    total, number = [
        jnp.sum(
            jnp.sum(
                functools.reduce(jnp.add, [ref[i] for ref in (sums_ref, *far_refs)]),
                axis=1,
                keepdims=True,
            ),
            axis=0,
            keepdims=True,
        )
        for i in range(2)
    ]
    variance = total / jnp.maximum(number, 1.0) + 1e-05
    h = smoothing_ref[0]
    inverse = 1.0 / (54.0 * h * h * variance)
    factor = jnp.broadcast_to(inverse * (-1.4426950408889634), (8, 128))

    def keep(y, new):
        steps.store(val, new, 4, y)

    def finish(y, new):
        for t, x in enumerate(ring.plain(new, cols // 128)):
            stage[t, pl.ds(y - HALO, 8, stride=rows), :] = x

    steps.run([OUT - 8], 8, 4, steps.early(factor))
    steps.run([OUT], full - 2 * OUT, 5, steps.combine(factor, keep))

    steps.run([OUT], full - 2 * OUT, 10, steps.prepare(4))
    steps.run([OUT + 1], full - 2 * OUT - 2, 8, steps.corrections)
    steps.run([low - 8], rows + 8, 8, steps.distances(APART))
    steps.run([low], rows, 8, steps.distances(LEVEL))
    steps.run([low - 8], 8, 4, steps.early(factor))
    steps.run([low], rows, 8, steps.combine(factor, finish))
    for t in range(cols // 128):
        out_ref[:, t * 128 : (t + 1) * 128] = stage[t]


def on_device(volume, tissue_mask, smoothing):
    depth, rows, cols = volume.shape
    blocks = tissue_mask.shape[1]
    count = rows + blocks
    lanes = cols + 128
    full = rows + 2 * HALO
    spans = blocks + 6
    vm = pl.BlockSpec(memory_space=VMEM)
    shape = lambda *s: jax.ShapeDtypeStruct(s, F32)
    params = pltpu.CompilerParams(vmem_limit_bytes=32 * 1024 * 1024)
    own, low, high, sums = pl.pallas_call(
        pack_kernel,
        out_shape=(
            shape(count, 8, cols),
            shape(count // 4 + 2, 8, 128),
            shape(count // 4 + 2, 8, 128),
            shape(2, 8, 128),
        ),
        in_specs=[vm, vm],
        out_specs=[vm] * 4,
        scratch_shapes=[pltpu.VMEM((depth * rows, 128), F32)],
        compiler_params=params,
        name="pack",
    )(volume.reshape(depth * rows, cols), tissue_mask)

    def ring(x, axis, by):
        size = lax.axis_size(axis)
        return lax.ppermute(x, axis, [(i, (i + by) % size) for i in range(size)])

    def line(x, axis, by):
        size = lax.axis_size(axis)
        return lax.ppermute(x, axis, [(i, i + by) for i in range(size) if 0 <= i + by < size])

    def beyond(x, axis):
        return [ring(x, axis, by) for by in range(2, lax.axis_size(axis) - 1)]

    def swap(x):
        return lax.ppermute(x, "gx", [(c, c ^ 1) for c in range(lax.axis_size("gx"))])

    def far_rows(x, ends):
        ny, nx = lax.axis_size("gy"), lax.axis_size("gx")
        shifts = list(range(2, ny - 1)) + [None]
        got = []
        for even, odd in zip(shifts[0::2], shifts[1::2]):
            pairs = []
            for y in range(ny):
                for c in range(nx):
                    by = odd if c % 2 else even
                    to = ny - 1 - y if by is None else (y + by) % ny
                    pairs.append((y * nx + c, to * nx + c))
            got.append(lax.ppermute(ends if odd is None else x, ("gy", "gx"), pairs))
        return functools.reduce(jnp.add, got)

    right = ring(low, "gx", -1)
    left = ring(high, "gx", 1)
    far = [] if lax.axis_size("gx") == 4 else beyond(sums, "gx")
    ordered = pl.pallas_call(
        order_kernel,
        out_shape=shape(count, 8, lanes),
        in_specs=[vm],
        out_specs=vm,
        compiler_params=params,
        cost_estimate=pl.CostEstimate(flops=5_000_000, bytes_accessed=1_000_000, transcendentals=0),
        name="order",
    )(own)
    half = pl.pallas_call(
        half_kernel,
        out_shape=shape(2, 8, 128),
        in_specs=[vm] * (3 + len(far)),
        out_specs=vm,
        compiler_params=params,
        name="half",
    )(left, right, sums, *far)
    other = swap(half)
    wide, top, bottom = pl.pallas_call(
        widen_kernel,
        out_shape=(
            shape(count, 8, lanes),
            shape(HALO + 2, 8, lanes),
            shape(HALO + 2, 8, lanes),
        ),
        in_specs=[vm] * 4,
        out_specs=[vm] * 3,
        input_output_aliases={0: 0},
        compiler_params=params,
        name="widen",
    )(ordered, left, right, half)
    below = line(top, "gy", -1)
    above = line(bottom, "gy", 1)
    state = [
        shape(5, full, 8, lanes),
        shape(3, full, 8, lanes),
        shape(len(FIELDS), full, 8, lanes),
        shape(4, spans, 8, lanes),
        shape(len(FIELDS), spans, 8, lanes),
    ]
    held = pl.pallas_call(
        inner_kernel,
        out_shape=state,
        in_specs=[vm],
        out_specs=[vm] * 5,
        compiler_params=params,
        cost_estimate=pl.CostEstimate(flops=20_000_000, bytes_accessed=8_000_000, transcendentals=0),
        name="inner",
    )(wide)
    other, *held = lax.optimization_barrier((other, *held))
    sums, ends = pl.pallas_call(
        whole_kernel,
        out_shape=[shape(2, 8, 128)] * 2,
        in_specs=[vm] * 2,
        out_specs=[vm] * 2,
        compiler_params=params,
        name="whole",
    )(half, other)
    far = far_rows(sums, ends)
    part, *held = pl.pallas_call(
        outer_kernel,
        out_shape=[shape(2, 8, 128)] + state,
        in_specs=[vm] * 7,
        out_specs=[vm] * 6,
        input_output_aliases={2 + i: 1 + i for i in range(5)},
        compiler_params=params,
        cost_estimate=pl.CostEstimate(flops=20_000_000, bytes_accessed=8_000_000, transcendentals=0),
        name="outer",
    )(above, below, *held)
    part, far = lax.optimization_barrier((part, far))
    far = [part, swap(part), far, swap(far)]
    out = pl.pallas_call(
        functools.partial(smooth_kernel, len(far)),
        out_shape=[shape(depth * rows, cols)] + state,
        in_specs=[vm] + [pl.BlockSpec(memory_space=pltpu.SMEM)] + [vm] * (len(far) + 5),
        out_specs=[vm] * 6,
        input_output_aliases={2 + len(far) + i: 1 + i for i in range(5)},
        scratch_shapes=[pltpu.VMEM((cols // 128, depth * rows, 128), F32)],
        compiler_params=params,
        name="smooth",
    )(sums, smoothing, *far, *held)[0]
    return out.reshape(depth, rows, cols)


def solution(mesh):
    placed = (P(None, ("slab", "gy"), "gx"), P(None, ("slab", "gy"), "gx"), P())
    return jax.shard_map(
        on_device,
        mesh=mesh,
        in_specs=placed,
        out_specs=P(None, ("slab", "gy"), "gx"),
        check_vma=False,
    )
```

```python
import functools

import jax
import jax.numpy as jnp
from jax import lax
from jax.experimental import pallas as pl
from jax.experimental.pallas import tpu as pltpu
from jax.sharding import PartitionSpec as P

F32 = jnp.float32
HALO = 18
OUT = HALO // 2
VMEM = pltpu.VMEM


def iotas():
    return (
        lax.broadcasted_iota(jnp.int32, (8, 128), 0),
        lax.broadcasted_iota(jnp.int32, (8, 128), 1),
    )


def lane_roll(x, by):
    return pltpu.roll(x, by % 128, 1)


def depth_roll(x, by):
    return pltpu.roll(x, by % 8, 0)


def picked(x, index):
    return jnp.take_along_axis(x, index, axis=1, mode="promise_in_bounds")


class Ring:
    def __init__(self, tiles):
        self.tiles = tiles
        lane = iotas()[1]
        self.lane = lane
        column = [lane * tiles + t for t in range(tiles)]
        self.index = [lax.rem(c, 128) for c in column]
        self.home = [lax.div(c, 128) for c in column]

    def own(self, x):
        result = []
        for index, home in zip(self.index, self.home):
            total = picked(x[0], index)
            for i in range(1, len(x)):
                total = jnp.where(home == i, picked(x[i], index), total)
            result.append(total)
        return result

    def edges(self, x, edge):
        last = self.tiles - 1
        return [
            jnp.where(home == last, picked(edge, index), v)
            for v, index, home in zip(x, self.index, self.home)
        ]

    def unpacked(self, left, right, group):
        edge = jnp.where(self.lane < HALO, lane_roll(right, -32 * group), 0.0)
        return jnp.where(self.lane >= 128 - HALO, lane_roll(left, 32 * (3 - group)), edge)

    def plain(self, x, count):
        result = []
        for t in range(count):
            column = self.lane + 128 * t
            index, home = lax.div(column, self.tiles), lax.rem(column, self.tiles)
            total = picked(x[0], index)
            for i in range(1, self.tiles):
                total = jnp.where(home == i, picked(x[i], index), total)
            result.append(total)
        return result


def split(ref, row, tiles):
    return [ref[row, :, t * 128 : (t + 1) * 128] for t in range(tiles)]


def put(ref, row, x):
    for t, v in enumerate(x):
        ref[row, :, t * 128 : (t + 1) * 128] = v


def pack_kernel(vol_ref, mask_ref, own_ref, low_ref, high_ref, sums_ref, stage):
    cols = own_ref.shape[2]
    rows = own_ref.shape[0] - mask_ref.shape[1]
    blocks = mask_ref.shape[1]
    tiles = cols // 128
    sub, lane = iotas()
    wide = lax.broadcasted_iota(jnp.int32, (mask_ref.shape[2], cols), 1) // 8
    spread = (wide == lax.broadcasted_iota(jnp.int32, wide.shape, 0)).astype(F32)
    half = lax.broadcasted_iota(jnp.int32, (8, mask_ref.shape[2]), 0) < 4
    tissue = []
    for b in range(blocks):
        picked = jnp.where(half, mask_ref[0, b : b + 1, :], mask_ref[1, b : b + 1, :])
        t = jnp.dot(picked.astype(F32), spread, preferred_element_type=F32)
        own_ref[rows + b] = t
        tissue.append(t)
    total = jnp.zeros((8, 128), F32)
    count = jnp.zeros((8, 128), F32)
    for t in range(tiles):
        sl = slice(t * 128, (t + 1) * 128)
        stage[...] = vol_ref[:, sl]
        for b in range(blocks):
            part = jnp.zeros((8, 128), F32)
            for y in range(b * 8, b * 8 + 8):
                v = stage[pl.ds(y, 8, stride=rows), :]
                own_ref[y, :, sl] = v
                res = v - 0.5 * (depth_roll(v, 1) + depth_roll(v, -1))
                part = part + res * res
            total = total + part * tissue[b][:, sl]
            count = count + tissue[b][:, sl]
    inner = (sub >= 1) & (sub <= 6)
    total = jnp.where(inner, total * (2.0 / 3.0), 0.0)
    count = jnp.where(inner, count * 8.0, 0.0)
    sums_ref[0] = total
    sums_ref[1] = count
    packs = (rows + blocks) // 4
    group = lane // 32
    for k in range(packs):
        low = own_ref[4 * k, :, 0:128]
        high = lane_roll(own_ref[4 * k, :, cols - 128 : cols], 32)
        for g in range(1, 4):
            low = jnp.where(group == g, lane_roll(own_ref[4 * k + g, :, 0:128], 32 * g), low)
            high = jnp.where(
                group == g, lane_roll(own_ref[4 * k + g, :, cols - 128 : cols], 32 * (g + 1)), high
            )
        low_ref[k] = low
        high_ref[k] = high
    for ref in (low_ref, high_ref):
        ref[packs] = total
        ref[packs + 1] = count


def half_kernel(left_ref, right_ref, own_ref, *refs):
    packs = left_ref.shape[0] - 2
    odd = lax.rem(lax.axis_index("gx"), 2).astype(F32)
    for i in range(2):
        left, right = left_ref[packs + i], right_ref[packs + i]
        if len(refs) == 1:
            refs[-1][i] = own_ref[i] + left * (1.0 - odd) + right * odd
        else:
            refs[-1][i] = 0.5 * functools.reduce(
                jnp.add, [ref[i] for ref in refs[:-1]], own_ref[i] + left + right
            )


def whole_kernel(half_ref, other_ref, sums_ref, ends_ref):
    place, last = lax.axis_index("gy"), lax.axis_size("gy") - 1
    at_end = ((place == 0) | (place == last)).astype(F32)
    for i in range(2):
        sums_ref[i] = half_ref[i] + other_ref[i]
        ends_ref[i] = sums_ref[i] * jnp.where(lax.rem(lax.axis_index("gx"), 2) == 0, 1.0, at_end)


def order_kernel(own_ref, wide_ref):
    tiles = own_ref.shape[2] // 128
    ring = Ring(tiles + 1)
    for i in range(own_ref.shape[0]):
        put(wide_ref, i, ring.own(split(own_ref, i, tiles)))


def widen_kernel(part_ref, left_ref, right_ref, half_ref, wide_ref, top_ref, bottom_ref):
    tiles = wide_ref.shape[2] // 128
    count = wide_ref.shape[0]
    rows = count - count // 9
    ring = Ring(tiles)
    place = lax.axis_index("gx")
    has_left = (place > 0).astype(F32)
    has_right = (place < lax.axis_size("gx") - 1).astype(F32)
    for k in range(count // 4):
        left = left_ref[k] * has_left
        right = right_ref[k] * has_right
        for g in range(4):
            i = 4 * k + g
            put(wide_ref, i, ring.edges(split(part_ref, i, tiles), ring.unpacked(left, right, g)))
    sub = iotas()[0]
    for ref, row, block in ((top_ref, 0, rows), (bottom_ref, rows - HALO, count - 3)):
        ref[0:HALO] = wide_ref[row : row + HALO]
        packed = [jnp.zeros((8, 128), F32)] * tiles
        for b in range(3):
            for i in range(2):
                some = [v[4 * i : 4 * i + 1] for v in split(wide_ref, block + b, tiles)]
                packed = [jnp.where(sub == 2 * b + i, x, y) for x, y in zip(some, packed)]
        put(ref, HALO, packed)
        put(ref, HALO + 1, [half_ref[0], half_ref[1]] + [packed[0]] * (tiles - 2))


FIELDS = [(0, 8), (1, -8), (1, 0), (1, 8), (2, 8), (2, 0), (3, -8), (3, 0), (3, 8)]
APART = [f for f, (_, step) in enumerate(FIELDS) if step]
LEVEL = [f for f, (_, step) in enumerate(FIELDS) if not step]


class Steps:
    def __init__(self, val, cor, dist, tis, pair):
        self.val, self.cor, self.dist, self.tis, self.pair = val, cor, dist, tis, pair
        self.tiles = val.shape[-1] // 128
        self.tile = [slice(t * 128, (t + 1) * 128) for t in range(self.tiles)]
        self.sub, self.lane = iotas()
        self.edge34 = (self.sub == 3) | (self.sub == 4)
        self.edge04 = (self.sub == 0) | (self.sub == 4)
        self.edge37 = (self.sub == 3) | (self.sub == 7)

    def load(self, ref, *idx):
        return [ref[(*idx, slice(None), s)] for s in self.tile]

    def store(self, ref, x, *idx):
        for t, s in enumerate(self.tile):
            ref[(*idx, slice(None), s)] = x[t]

    def along(self, x, by):
        moved = []
        for j in range(self.tiles):
            lanes, source = divmod(j + by, self.tiles)
            moved.append(lane_roll(x[source], -lanes) if lanes else x[source])
        return moved

    def box_lanes(self, x):
        down, up = self.along(x, -1), self.along(x, 1)
        first = x[0] + up[0]
        second = first + up[1]
        return [first + down[0], second] + [
            (x[t] + down[t]) + up[t] for t in range(2, self.tiles)
        ]

    def box_rows(self, e):
        result = []
        for i in range(0, len(e) - 2, 2):
            middle = [a + b for a, b in zip(e[i + 1], e[i + 2])]
            result.append([a + b for a, b in zip(e[i], middle)])
            if i + 3 < len(e):
                result.append([a + b for a, b in zip(middle, e[i + 3])])
        return result

    def run(self, starts, number, group, fn):
        whole = number // group
        if whole:
            @pl.loop(0, whole)
            def _(i):
                for start in starts:
                    fn(start + i * group, group)
        if number % group:
            for start in starts:
                fn(start + whole * group, number % group)

    def tissue(self, spans):
        for b in spans:
            t0 = self.load(self.tis, 0, b)
            t1 = self.along(t0, 8)
            self.store(self.tis, t1, 1, b)
            self.store(self.tis, [depth_roll(v, 4) for v in t0], 2, b)
            self.store(self.tis, [depth_roll(v, 4) for v in t1], 3, b)

    def pairs(self, spans, level_spans):
        for f, (kind, step) in enumerate(FIELDS):
            for b in spans if step else level_spans:
                low, high = b, b + (1 if step else 0)
                p, q = (high, low) if step < 0 else (low, high)
                for s in self.tile:
                    self.pair[f, b, :, s] = self.tis[0, p, :, s] * self.tis[kind, q, :, s]

    def prepare(self, source):
        def fn(r, group):
            for i in range(group):
                v = self.load(self.val, source, r + i)
                v8 = self.along(v, 8)
                if source:
                    self.store(self.val, v, 0, r + i)
                self.store(self.val, v8, 1, r + i)
                self.store(self.val, [depth_roll(x, 4) for x in v], 2, r + i)
                self.store(self.val, [depth_roll(x, 4) for x in v8], 3, r + i)

        return fn

    def corrections(self, r, group):
        square = []
        for i in range(-1, group + 1):
            square.append([x * x for x in self.load(self.val, 0, r + i)])
        sums = self.box_rows(square)
        for base in range(0, group, 4):
            some = sums[base : base + 4]
            packed = [depth_roll(x, 4) for x in some[0]]
            for i, row in enumerate(some):
                for place, by in ((2 * i, 2 * i - 4), (2 * i + 1, 2 * i - 2)):
                    if place:
                        here = self.sub == place
                        packed = [
                            jnp.where(here, depth_roll(x, by), y) for x, y in zip(row, packed)
                        ]
            packed = self.box_lanes(packed)
            moved = self.along(packed, 8)
            for i in range(len(some)):
                y = r + base + i
                self.store(self.cor, [depth_roll(x, 3 - 2 * i) for x in packed], 0, y)
                self.store(self.cor, [depth_roll(x, 7 - 2 * i) for x in packed], 1, y)
                self.store(self.cor, [depth_roll(x, 7 - 2 * i) for x in moved], 2, y)

    def distances(self, fields):
        def fn(r, group):
            shared = {}
            for f in fields:
                kind, step = FIELDS[f]
                p = r + 8 if step < 0 else r
                q = r + 8 if step > 0 else r
                if (step < 0) not in shared:
                    shared[step < 0] = [
                        self.load(self.val, 0, p + i) for i in range(-1, group + 1)
                    ]
                e = []
                for i in range(-1, group + 1):
                    other = self.load(self.val, kind, q + i)
                    d = [a - b for a, b in zip(shared[step < 0][i + 1], other)]
                    e.append([x * x for x in d])
                for i, s in enumerate(self.box_rows(e)):
                    s = self.box_lanes(s)
                    up = [depth_roll(x, 1) for x in s]
                    down = [depth_roll(x, -1) for x in s]
                    if kind >= 2:
                        near = self.load(self.cor, 0, p + i)
                        far = self.load(self.cor, kind - 1, q + i)
                        c = [jnp.where(self.edge34, a, b) for a, b in zip(near, far)]
                        up = [jnp.where(self.edge04, a, b) for a, b in zip(c, up)]
                        down = [jnp.where(self.edge37, a, b) for a, b in zip(c, down)]
                    else:
                        up = [jnp.where(self.sub == 0, 0.0, b) for b in up]
                        down = [jnp.where(self.sub == 7, 0.0, b) for b in down]
                    self.store(
                        self.dist, [a + b + c for a, b, c in zip(s, up, down)], f, r + i
                    )

        return fn

    def weight(self, f, r, factor):
        both = self.load(self.pair, f, (r + 24 - HALO) // 8)
        d = self.load(self.dist, f, r)
        return [jnp.exp2(a * factor) * b for a, b in zip(d, both)]

    def early(self, factor):
        def fn(r, group):
            for i in range(group):
                for f in APART:
                    self.store(self.dist, self.weight(f, r + i, factor), f, r + i)

        return fn

    def combine(self, factor, put):
        def fn(r, group):
            for i in range(group):
                y = r + i
                centre = self.load(self.val, 0, y)
                own = self.load(self.tis, 0, (y + 24 - HALO) // 8)
                den = [None] * 4
                num = [None] * 4

                def add(frame, w, v):
                    if den[frame] is None:
                        den[frame] = list(w)
                        num[frame] = [a * b for a, b in zip(w, v)]
                    else:
                        den[frame] = [a + b for a, b in zip(den[frame], w)]
                        num[frame] = [n + a * b for n, a, b in zip(num[frame], w, v)]

                for f, (kind, step) in enumerate(FIELDS):
                    w = self.weight(f, y, factor)
                    before = w
                    if step:
                        before = self.load(self.dist, f, y - 8)
                        self.store(self.dist, w, f, y)
                    at_p, at_q = (before, w) if step < 0 else (w, before)
                    add(0, at_p, self.load(self.val, kind, y + step))
                    if (kind, step) != (2, 0):
                        add(kind, at_q, self.load(self.val, 0, y - step))
                result = []
                for acc in (den, num):
                    side = [a + depth_roll(b, 4) for a, b in zip(acc[1], acc[3])]
                    side = self.along(side, -8)
                    result.append(
                        [a + depth_roll(b, 4) + c for a, b, c in zip(acc[0], acc[2], side)]
                    )
                new = []
                for t in range(self.tiles):
                    n, d = result[1][t] + centre[t], result[0][t] + 1.0
                    new.append(jnp.where(own[t] > 0.0, n / d, centre[t]))
                put(y, new)

        return fn


def inner_kernel(wide_ref, val, cor, dist, tis, pair):
    count = wide_ref.shape[0]
    blocks = count // 9
    rows = count - blocks
    low, high = HALO, HALO + rows
    steps = Steps(val, cor, dist, tis, pair)
    val[0, low:high] = wide_ref[0:rows]
    tis[0, 3 : 3 + blocks] = wide_ref[rows:count]
    steps.tissue(range(3, 3 + blocks))
    steps.pairs(range(3, 2 + blocks), range(3, 3 + blocks))
    steps.run([low], rows, 16, steps.prepare(0))
    steps.run([low + 1], rows - 2, 15, steps.corrections)
    steps.run([low + 1], rows - 10, 11, steps.distances(APART))
    steps.run([low + 1], rows - 2, 10, steps.distances(LEVEL))


def outer_kernel(above_ref, below_ref, *refs):
    part_ref, val, cor, dist, tis, pair = refs[5:]
    full = val.shape[1]
    rows = full - 2 * HALO
    spans = tis.shape[1]
    low, high = HALO, HALO + rows
    steps = Steps(val, cor, dist, tis, pair)

    for ref, row, block in ((above_ref, 0, 0), (below_ref, high, spans - 3)):
        val[0, row : row + HALO] = ref[0:HALO]
        packed = split(ref, HALO, steps.tiles)
        for b in range(3):
            steps.store(
                tis,
                [
                    jnp.where(steps.sub < 4, v[2 * b : 2 * b + 1], v[2 * b + 1 : 2 * b + 2])
                    for v in packed
                ],
                0,
                block + b,
            )
    ends = [*range(0, 3), *range(spans - 3, spans)]
    steps.tissue(ends)
    steps.pairs([*range(0, 3), *range(spans - 4, spans - 1)], ends)
    for i in range(2):
        lanes = slice(i * 128, (i + 1) * 128)
        part_ref[i] = above_ref[HALO + 1, :, lanes] + below_ref[HALO + 1, :, lanes]

    steps.run([0, high], HALO, 18, steps.prepare(0))
    steps.run([1, high - 1], HALO, 18, steps.corrections)
    steps.run([OUT - 8, high - 9], low + 1 - (OUT - 8), 9, steps.distances(APART))
    steps.run([OUT, high - 1], low + 1 - OUT, 10, steps.distances(LEVEL))


def smooth_kernel(fars, sums_ref, smoothing_ref, *refs):
    far_refs, refs = refs[:fars], refs[fars + 5 :]
    out_ref, val, cor, dist, tis, pair, stage = refs
    cols = out_ref.shape[1]
    full = val.shape[1]
    rows = full - 2 * HALO
    low = HALO
    steps = Steps(val, cor, dist, tis, pair)
    ring = Ring(steps.tiles)

    total, number = [
        jnp.sum(
            jnp.sum(
                functools.reduce(jnp.add, [ref[i] for ref in (sums_ref, *far_refs)]),
                axis=1,
                keepdims=True,
            ),
            axis=0,
            keepdims=True,
        )
        for i in range(2)
    ]
    variance = total / jnp.maximum(number, 1.0) + 1e-05
    h = smoothing_ref[0]
    inverse = 1.0 / (54.0 * h * h * variance)
    factor = jnp.broadcast_to(inverse * (-1.4426950408889634), (8, 128))

    def keep(y, new):
        steps.store(val, new, 4, y)

    def finish(y, new):
        for t, x in enumerate(ring.plain(new, cols // 128)):
            stage[t, pl.ds(y - HALO, 8, stride=rows), :] = x

    steps.run([OUT - 8], 8, 8, steps.early(factor))
    steps.run([OUT], full - 2 * OUT, 5, steps.combine(factor, keep))

    steps.run([OUT], full - 2 * OUT, 25, steps.prepare(4))
    steps.run([OUT + 1], full - 2 * OUT - 2, 16, steps.corrections)
    steps.run([low - 8], rows + 8, 10, steps.distances(APART))
    steps.run([low], rows, 8, steps.distances(LEVEL))
    steps.run([low - 8], 8, 8, steps.early(factor))
    steps.run([low], rows, 8, steps.combine(factor, finish))
    for t in range(cols // 128):
        out_ref[:, t * 128 : (t + 1) * 128] = stage[t]


def on_device(volume, tissue_mask, smoothing):
    depth, rows, cols = volume.shape
    blocks = tissue_mask.shape[1]
    count = rows + blocks
    lanes = cols + 128
    full = rows + 2 * HALO
    spans = blocks + 6
    vm = pl.BlockSpec(memory_space=VMEM)
    shape = lambda *s: jax.ShapeDtypeStruct(s, F32)
    params = pltpu.CompilerParams(vmem_limit_bytes=32 * 1024 * 1024)
    own, low, high, sums = pl.pallas_call(
        pack_kernel,
        out_shape=(
            shape(count, 8, cols),
            shape(count // 4 + 2, 8, 128),
            shape(count // 4 + 2, 8, 128),
            shape(2, 8, 128),
        ),
        in_specs=[vm, vm],
        out_specs=[vm] * 4,
        scratch_shapes=[pltpu.VMEM((depth * rows, 128), F32)],
        compiler_params=params,
        name="pack",
    )(volume.reshape(depth * rows, cols), tissue_mask)

    def ring(x, axis, by):
        size = lax.axis_size(axis)
        return lax.ppermute(x, axis, [(i, (i + by) % size) for i in range(size)])

    def line(x, axis, by):
        size = lax.axis_size(axis)
        return lax.ppermute(x, axis, [(i, i + by) for i in range(size) if 0 <= i + by < size])

    def beyond(x, axis):
        return [ring(x, axis, by) for by in range(2, lax.axis_size(axis) - 1)]

    def swap(x):
        return lax.ppermute(x, "gx", [(c, c ^ 1) for c in range(lax.axis_size("gx"))])

    def far_rows(x, ends):
        ny, nx = lax.axis_size("gy"), lax.axis_size("gx")
        shifts = list(range(2, ny - 1)) + [None]
        got = []
        for even, odd in zip(shifts[0::2], shifts[1::2]):
            pairs = []
            for y in range(ny):
                for c in range(nx):
                    by = odd if c % 2 else even
                    to = ny - 1 - y if by is None else (y + by) % ny
                    pairs.append((y * nx + c, to * nx + c))
            got.append(lax.ppermute(ends if odd is None else x, ("gy", "gx"), pairs))
        return functools.reduce(jnp.add, got)

    right = ring(low, "gx", -1)
    left = ring(high, "gx", 1)
    far = [] if lax.axis_size("gx") == 4 else beyond(sums, "gx")
    ordered = pl.pallas_call(
        order_kernel,
        out_shape=shape(count, 8, lanes),
        in_specs=[vm],
        out_specs=vm,
        compiler_params=params,
        cost_estimate=pl.CostEstimate(flops=5_000_000, bytes_accessed=1_000_000, transcendentals=0),
        name="order",
    )(own)
    half = pl.pallas_call(
        half_kernel,
        out_shape=shape(2, 8, 128),
        in_specs=[vm] * (3 + len(far)),
        out_specs=vm,
        compiler_params=params,
        name="half",
    )(left, right, sums, *far)
    other = swap(half)
    wide, top, bottom = pl.pallas_call(
        widen_kernel,
        out_shape=(
            shape(count, 8, lanes),
            shape(HALO + 2, 8, lanes),
            shape(HALO + 2, 8, lanes),
        ),
        in_specs=[vm] * 4,
        out_specs=[vm] * 3,
        input_output_aliases={0: 0},
        compiler_params=params,
        name="widen",
    )(ordered, left, right, half)
    below = line(top, "gy", -1)
    above = line(bottom, "gy", 1)
    state = [
        shape(5, full, 8, lanes),
        shape(3, full, 8, lanes),
        shape(len(FIELDS), full, 8, lanes),
        shape(4, spans, 8, lanes),
        shape(len(FIELDS), spans, 8, lanes),
    ]
    held = pl.pallas_call(
        inner_kernel,
        out_shape=state,
        in_specs=[vm],
        out_specs=[vm] * 5,
        compiler_params=params,
        cost_estimate=pl.CostEstimate(flops=20_000_000, bytes_accessed=8_000_000, transcendentals=0),
        name="inner",
    )(wide)
    other, *held = lax.optimization_barrier((other, *held))
    sums, ends = pl.pallas_call(
        whole_kernel,
        out_shape=[shape(2, 8, 128)] * 2,
        in_specs=[vm] * 2,
        out_specs=[vm] * 2,
        compiler_params=params,
        name="whole",
    )(half, other)
    far = far_rows(sums, ends)
    part, *held = pl.pallas_call(
        outer_kernel,
        out_shape=[shape(2, 8, 128)] + state,
        in_specs=[vm] * 7,
        out_specs=[vm] * 6,
        input_output_aliases={2 + i: 1 + i for i in range(5)},
        compiler_params=params,
        cost_estimate=pl.CostEstimate(flops=20_000_000, bytes_accessed=8_000_000, transcendentals=0),
        name="outer",
    )(above, below, *held)
    part, far = lax.optimization_barrier((part, far))
    far = [part, swap(part), far, swap(far)]
    out = pl.pallas_call(
        functools.partial(smooth_kernel, len(far)),
        out_shape=[shape(depth * rows, cols)] + state,
        in_specs=[vm] + [pl.BlockSpec(memory_space=pltpu.SMEM)] + [vm] * (len(far) + 5),
        out_specs=[vm] * 6,
        input_output_aliases={2 + len(far) + i: 1 + i for i in range(5)},
        scratch_shapes=[pltpu.VMEM((cols // 128, depth * rows, 128), F32)],
        compiler_params=params,
        name="smooth",
    )(sums, smoothing, *far, *held)[0]
    return out.reshape(depth, rows, cols)


def solution(mesh):
    placed = (P(None, ("slab", "gy"), "gx"), P(None, ("slab", "gy"), "gx"), P())
    return jax.shard_map(
        on_device,
        mesh=mesh,
        in_specs=placed,
        out_specs=P(None, ("slab", "gy"), "gx"),
        check_vma=False,
    )
```

```python
import functools

import jax
import jax.numpy as jnp
from jax import lax
from jax.experimental import pallas as pl
from jax.experimental.pallas import tpu as pltpu
from jax.sharding import PartitionSpec as P

F32 = jnp.float32
HALO = 18
OUT = HALO // 2
VMEM = pltpu.VMEM


def iotas():
    return (
        lax.broadcasted_iota(jnp.int32, (8, 128), 0),
        lax.broadcasted_iota(jnp.int32, (8, 128), 1),
    )


def lane_roll(x, by):
    return pltpu.roll(x, by % 128, 1)


def depth_roll(x, by):
    return pltpu.roll(x, by % 8, 0)


def picked(x, index):
    return jnp.take_along_axis(x, index, axis=1, mode="promise_in_bounds")


class Ring:
    def __init__(self, tiles):
        self.tiles = tiles
        lane = iotas()[1]
        self.lane = lane
        column = [lane * tiles + t for t in range(tiles)]
        self.index = [lax.rem(c, 128) for c in column]
        self.home = [lax.div(c, 128) for c in column]

    def own(self, x):
        result = []
        for index, home in zip(self.index, self.home):
            total = picked(x[0], index)
            for i in range(1, len(x)):
                total = jnp.where(home == i, picked(x[i], index), total)
            result.append(total)
        return result

    def edges(self, x, edge):
        last = self.tiles - 1
        return [
            jnp.where(home == last, picked(edge, index), v)
            for v, index, home in zip(x, self.index, self.home)
        ]

    def unpacked(self, left, right, group):
        edge = jnp.where(self.lane < HALO, lane_roll(right, -32 * group), 0.0)
        return jnp.where(self.lane >= 128 - HALO, lane_roll(left, 32 * (3 - group)), edge)

    def plain(self, x, count):
        result = []
        for t in range(count):
            column = self.lane + 128 * t
            index, home = lax.div(column, self.tiles), lax.rem(column, self.tiles)
            total = picked(x[0], index)
            for i in range(1, self.tiles):
                total = jnp.where(home == i, picked(x[i], index), total)
            result.append(total)
        return result


def split(ref, row, tiles):
    return [ref[row, :, t * 128 : (t + 1) * 128] for t in range(tiles)]


def put(ref, row, x):
    for t, v in enumerate(x):
        ref[row, :, t * 128 : (t + 1) * 128] = v


def pack_kernel(vol_ref, mask_ref, own_ref, low_ref, high_ref, sums_ref, stage):
    cols = own_ref.shape[2]
    rows = own_ref.shape[0] - mask_ref.shape[1]
    blocks = mask_ref.shape[1]
    tiles = cols // 128
    sub, lane = iotas()
    wide = lax.broadcasted_iota(jnp.int32, (mask_ref.shape[2], cols), 1) // 8
    spread = (wide == lax.broadcasted_iota(jnp.int32, wide.shape, 0)).astype(F32)
    half = lax.broadcasted_iota(jnp.int32, (8, mask_ref.shape[2]), 0) < 4
    tissue = []
    for b in range(blocks):
        picked = jnp.where(half, mask_ref[0, b : b + 1, :], mask_ref[1, b : b + 1, :])
        t = jnp.dot(picked.astype(F32), spread, preferred_element_type=F32)
        own_ref[rows + b] = t
        tissue.append(t)
    total = jnp.zeros((8, 128), F32)
    count = jnp.zeros((8, 128), F32)
    for t in range(tiles):
        sl = slice(t * 128, (t + 1) * 128)
        stage[...] = vol_ref[:, sl]
        for b in range(blocks):
            part = jnp.zeros((8, 128), F32)
            for y in range(b * 8, b * 8 + 8):
                v = stage[pl.ds(y, 8, stride=rows), :]
                own_ref[y, :, sl] = v
                res = v - 0.5 * (depth_roll(v, 1) + depth_roll(v, -1))
                part = part + res * res
            total = total + part * tissue[b][:, sl]
            count = count + tissue[b][:, sl]
    inner = (sub >= 1) & (sub <= 6)
    total = jnp.where(inner, total * (2.0 / 3.0), 0.0)
    count = jnp.where(inner, count * 8.0, 0.0)
    sums_ref[0] = total
    sums_ref[1] = count
    packs = (rows + blocks) // 4
    group = lane // 32
    for k in range(packs):
        low = own_ref[4 * k, :, 0:128]
        high = lane_roll(own_ref[4 * k, :, cols - 128 : cols], 32)
        for g in range(1, 4):
            low = jnp.where(group == g, lane_roll(own_ref[4 * k + g, :, 0:128], 32 * g), low)
            high = jnp.where(
                group == g, lane_roll(own_ref[4 * k + g, :, cols - 128 : cols], 32 * (g + 1)), high
            )
        low_ref[k] = low
        high_ref[k] = high
    for ref in (low_ref, high_ref):
        ref[packs] = total
        ref[packs + 1] = count


def half_kernel(left_ref, right_ref, own_ref, *refs):
    packs = left_ref.shape[0] - 2
    odd = lax.rem(lax.axis_index("gx"), 2).astype(F32)
    for i in range(2):
        left, right = left_ref[packs + i], right_ref[packs + i]
        if len(refs) == 1:
            refs[-1][i] = own_ref[i] + left * (1.0 - odd) + right * odd
        else:
            refs[-1][i] = 0.5 * functools.reduce(
                jnp.add, [ref[i] for ref in refs[:-1]], own_ref[i] + left + right
            )


def add_kernel(a_ref, b_ref, out_ref):
    out_ref[...] = a_ref[...] + b_ref[...]


def order_kernel(own_ref, wide_ref):
    tiles = own_ref.shape[2] // 128
    ring = Ring(tiles + 1)
    for i in range(own_ref.shape[0]):
        put(wide_ref, i, ring.own(split(own_ref, i, tiles)))


def widen_kernel(part_ref, left_ref, right_ref, wide_ref, top_ref, bottom_ref):
    tiles = wide_ref.shape[2] // 128
    count = wide_ref.shape[0]
    rows = count - count // 9
    ring = Ring(tiles)
    place = lax.axis_index("gx")
    has_left = (place > 0).astype(F32)
    has_right = (place < lax.axis_size("gx") - 1).astype(F32)
    for k in range(count // 4):
        left = left_ref[k] * has_left
        right = right_ref[k] * has_right
        for g in range(4):
            i = 4 * k + g
            put(wide_ref, i, ring.edges(split(part_ref, i, tiles), ring.unpacked(left, right, g)))
    sub = iotas()[0]
    for ref, row, block in ((top_ref, 0, rows), (bottom_ref, rows - HALO, count - 3)):
        ref[0:HALO] = wide_ref[row : row + HALO]
        packed = [jnp.zeros((8, 128), F32)] * tiles
        for b in range(3):
            for i in range(2):
                some = [v[4 * i : 4 * i + 1] for v in split(wide_ref, block + b, tiles)]
                packed = [jnp.where(sub == 2 * b + i, x, y) for x, y in zip(some, packed)]
        put(ref, HALO, packed)


FIELDS = [(0, 8), (1, -8), (1, 0), (1, 8), (2, 8), (2, 0), (3, -8), (3, 0), (3, 8)]
APART = [f for f, (_, step) in enumerate(FIELDS) if step]
LEVEL = [f for f, (_, step) in enumerate(FIELDS) if not step]


class Steps:
    def __init__(self, val, cor, dist, tis, pair):
        self.val, self.cor, self.dist, self.tis, self.pair = val, cor, dist, tis, pair
        self.tiles = val.shape[-1] // 128
        self.tile = [slice(t * 128, (t + 1) * 128) for t in range(self.tiles)]
        self.sub, self.lane = iotas()
        self.edge34 = (self.sub == 3) | (self.sub == 4)
        self.edge04 = (self.sub == 0) | (self.sub == 4)
        self.edge37 = (self.sub == 3) | (self.sub == 7)

    def load(self, ref, *idx):
        return [ref[(*idx, slice(None), s)] for s in self.tile]

    def store(self, ref, x, *idx):
        for t, s in enumerate(self.tile):
            ref[(*idx, slice(None), s)] = x[t]

    def along(self, x, by):
        moved = []
        for j in range(self.tiles):
            lanes, source = divmod(j + by, self.tiles)
            moved.append(lane_roll(x[source], -lanes) if lanes else x[source])
        return moved

    def box_lanes(self, x):
        down, up = self.along(x, -1), self.along(x, 1)
        first = x[0] + up[0]
        second = first + up[1]
        return [first + down[0], second] + [
            (x[t] + down[t]) + up[t] for t in range(2, self.tiles)
        ]

    def box_rows(self, e):
        result = []
        for i in range(0, len(e) - 2, 2):
            middle = [a + b for a, b in zip(e[i + 1], e[i + 2])]
            result.append([a + b for a, b in zip(e[i], middle)])
            if i + 3 < len(e):
                result.append([a + b for a, b in zip(middle, e[i + 3])])
        return result

    def run(self, starts, number, group, fn):
        whole = number // group
        if whole:
            @pl.loop(0, whole)
            def _(i):
                for start in starts:
                    fn(start + i * group, group)
        if number % group:
            for start in starts:
                fn(start + whole * group, number % group)

    def tissue(self, spans):
        for b in spans:
            t0 = self.load(self.tis, 0, b)
            t1 = self.along(t0, 8)
            self.store(self.tis, t1, 1, b)
            self.store(self.tis, [depth_roll(v, 4) for v in t0], 2, b)
            self.store(self.tis, [depth_roll(v, 4) for v in t1], 3, b)

    def pairs(self, spans, level_spans):
        for f, (kind, step) in enumerate(FIELDS):
            for b in spans if step else level_spans:
                low, high = b, b + (1 if step else 0)
                p, q = (high, low) if step < 0 else (low, high)
                for s in self.tile:
                    self.pair[f, b, :, s] = self.tis[0, p, :, s] * self.tis[kind, q, :, s]

    def prepare(self, source):
        def fn(r, group):
            for i in range(group):
                v = self.load(self.val, source, r + i)
                v8 = self.along(v, 8)
                if source:
                    self.store(self.val, v, 0, r + i)
                self.store(self.val, v8, 1, r + i)
                self.store(self.val, [depth_roll(x, 4) for x in v], 2, r + i)
                self.store(self.val, [depth_roll(x, 4) for x in v8], 3, r + i)

        return fn

    def corrections(self, r, group):
        square = []
        for i in range(-1, group + 1):
            square.append([x * x for x in self.load(self.val, 0, r + i)])
        sums = self.box_rows(square)
        for base in range(0, group, 4):
            some = sums[base : base + 4]
            packed = [depth_roll(x, 4) for x in some[0]]
            for i, row in enumerate(some):
                for place, by in ((2 * i, 2 * i - 4), (2 * i + 1, 2 * i - 2)):
                    if place:
                        here = self.sub == place
                        packed = [
                            jnp.where(here, depth_roll(x, by), y) for x, y in zip(row, packed)
                        ]
            packed = self.box_lanes(packed)
            moved = self.along(packed, 8)
            for i in range(len(some)):
                y = r + base + i
                self.store(self.cor, [depth_roll(x, 3 - 2 * i) for x in packed], 0, y)
                self.store(self.cor, [depth_roll(x, 7 - 2 * i) for x in packed], 1, y)
                self.store(self.cor, [depth_roll(x, 7 - 2 * i) for x in moved], 2, y)

    def distances(self, fields):
        def fn(r, group):
            shared = {}
            for f in fields:
                kind, step = FIELDS[f]
                p = r + 8 if step < 0 else r
                q = r + 8 if step > 0 else r
                if (step < 0) not in shared:
                    shared[step < 0] = [
                        self.load(self.val, 0, p + i) for i in range(-1, group + 1)
                    ]
                e = []
                for i in range(-1, group + 1):
                    other = self.load(self.val, kind, q + i)
                    d = [a - b for a, b in zip(shared[step < 0][i + 1], other)]
                    e.append([x * x for x in d])
                for i, s in enumerate(self.box_rows(e)):
                    s = self.box_lanes(s)
                    up = [depth_roll(x, 1) for x in s]
                    down = [depth_roll(x, -1) for x in s]
                    if kind >= 2:
                        near = self.load(self.cor, 0, p + i)
                        far = self.load(self.cor, kind - 1, q + i)
                        c = [jnp.where(self.edge34, a, b) for a, b in zip(near, far)]
                        up = [jnp.where(self.edge04, a, b) for a, b in zip(c, up)]
                        down = [jnp.where(self.edge37, a, b) for a, b in zip(c, down)]
                    else:
                        up = [jnp.where(self.sub == 0, 0.0, b) for b in up]
                        down = [jnp.where(self.sub == 7, 0.0, b) for b in down]
                    self.store(
                        self.dist, [a + b + c for a, b, c in zip(s, up, down)], f, r + i
                    )

        return fn

    def weight(self, f, r, factor):
        both = self.load(self.pair, f, (r + 24 - HALO) // 8)
        d = self.load(self.dist, f, r)
        return [jnp.exp2(a * factor) * b for a, b in zip(d, both)]

    def early(self, factor):
        def fn(r, group):
            for i in range(group):
                for f in APART:
                    self.store(self.dist, self.weight(f, r + i, factor), f, r + i)

        return fn

    def combine(self, factor, put):
        def fn(r, group):
            for i in range(group):
                y = r + i
                centre = self.load(self.val, 0, y)
                own = self.load(self.tis, 0, (y + 24 - HALO) // 8)
                den = [None] * 4
                num = [None] * 4

                def add(frame, w, v):
                    if den[frame] is None:
                        den[frame] = list(w)
                        num[frame] = [a * b for a, b in zip(w, v)]
                    else:
                        den[frame] = [a + b for a, b in zip(den[frame], w)]
                        num[frame] = [n + a * b for n, a, b in zip(num[frame], w, v)]

                for f, (kind, step) in enumerate(FIELDS):
                    w = self.weight(f, y, factor)
                    before = w
                    if step:
                        before = self.load(self.dist, f, y - 8)
                        self.store(self.dist, w, f, y)
                    at_p, at_q = (before, w) if step < 0 else (w, before)
                    add(0, at_p, self.load(self.val, kind, y + step))
                    if (kind, step) != (2, 0):
                        add(kind, at_q, self.load(self.val, 0, y - step))
                result = []
                for acc in (den, num):
                    side = [a + depth_roll(b, 4) for a, b in zip(acc[1], acc[3])]
                    side = self.along(side, -8)
                    result.append(
                        [a + depth_roll(b, 4) + c for a, b, c in zip(acc[0], acc[2], side)]
                    )
                new = []
                for t in range(self.tiles):
                    n, d = result[1][t] + centre[t], result[0][t] + 1.0
                    new.append(jnp.where(own[t] > 0.0, n / d, centre[t]))
                put(y, new)

        return fn


def inner_kernel(wide_ref, val, cor, dist, tis, pair):
    count = wide_ref.shape[0]
    blocks = count // 9
    rows = count - blocks
    low, high = HALO, HALO + rows
    steps = Steps(val, cor, dist, tis, pair)
    val[0, low:high] = wide_ref[0:rows]
    tis[0, 3 : 3 + blocks] = wide_ref[rows:count]
    steps.tissue(range(3, 3 + blocks))
    steps.pairs(range(3, 2 + blocks), range(3, 3 + blocks))
    steps.run([low], rows, 16, steps.prepare(0))
    steps.run([low + 1], rows - 2, 15, steps.corrections)
    steps.run([low + 1], rows - 10, 11, steps.distances(APART))
    steps.run([low + 1], rows - 2, 10, steps.distances(LEVEL))


def outer_kernel(above_ref, below_ref, *refs):
    val, cor, dist, tis, pair = refs[5:]
    full = val.shape[1]
    rows = full - 2 * HALO
    spans = tis.shape[1]
    low, high = HALO, HALO + rows
    steps = Steps(val, cor, dist, tis, pair)

    for ref, row, block in ((above_ref, 0, 0), (below_ref, high, spans - 3)):
        val[0, row : row + HALO] = ref[0:HALO]
        packed = split(ref, HALO, steps.tiles)
        for b in range(3):
            steps.store(
                tis,
                [
                    jnp.where(steps.sub < 4, v[2 * b : 2 * b + 1], v[2 * b + 1 : 2 * b + 2])
                    for v in packed
                ],
                0,
                block + b,
            )
    ends = [*range(0, 3), *range(spans - 3, spans)]
    steps.tissue(ends)
    steps.pairs([*range(0, 3), *range(spans - 4, spans - 1)], ends)
    steps.run([0, high], HALO, 18, steps.prepare(0))
    steps.run([1, high - 1], HALO, 18, steps.corrections)
    steps.run([OUT - 8, high - 9], low + 1 - (OUT - 8), 9, steps.distances(APART))
    steps.run([OUT, high - 1], low + 1 - OUT, 10, steps.distances(LEVEL))


def smooth_kernel(fars, sums_ref, smoothing_ref, *refs):
    far_refs, refs = refs[:fars], refs[fars + 5 :]
    out_ref, val, cor, dist, tis, pair, stage = refs
    cols = out_ref.shape[1]
    full = val.shape[1]
    rows = full - 2 * HALO
    low = HALO
    steps = Steps(val, cor, dist, tis, pair)
    ring = Ring(steps.tiles)

    total, number = [
        jnp.sum(
            jnp.sum(
                functools.reduce(jnp.add, [ref[i] for ref in (sums_ref, *far_refs)]),
                axis=1,
                keepdims=True,
            ),
            axis=0,
            keepdims=True,
        )
        for i in range(2)
    ]
    variance = total / jnp.maximum(number, 1.0) + 1e-05
    h = smoothing_ref[0]
    inverse = 1.0 / (54.0 * h * h * variance)
    factor = jnp.broadcast_to(inverse * (-1.4426950408889634), (8, 128))

    def keep(y, new):
        steps.store(val, new, 4, y)

    def finish(y, new):
        for t, x in enumerate(ring.plain(new, cols // 128)):
            stage[t, pl.ds(y - HALO, 8, stride=rows), :] = x

    steps.run([OUT - 8], 8, 8, steps.early(factor))
    steps.run([OUT], full - 2 * OUT, 5, steps.combine(factor, keep))

    steps.run([OUT], full - 2 * OUT, 25, steps.prepare(4))
    steps.run([OUT + 1], full - 2 * OUT - 2, 16, steps.corrections)
    steps.run([low - 8], rows + 8, 10, steps.distances(APART))
    steps.run([low], rows, 8, steps.distances(LEVEL))
    steps.run([low - 8], 8, 8, steps.early(factor))
    steps.run([low], rows, 8, steps.combine(factor, finish))
    for t in range(cols // 128):
        out_ref[:, t * 128 : (t + 1) * 128] = stage[t]


def on_device(volume, tissue_mask, smoothing):
    depth, rows, cols = volume.shape
    blocks = tissue_mask.shape[1]
    count = rows + blocks
    lanes = cols + 128
    full = rows + 2 * HALO
    spans = blocks + 6
    vm = pl.BlockSpec(memory_space=VMEM)
    shape = lambda *s: jax.ShapeDtypeStruct(s, F32)
    params = pltpu.CompilerParams(vmem_limit_bytes=32 * 1024 * 1024)
    own, low, high, sums = pl.pallas_call(
        pack_kernel,
        out_shape=(
            shape(count, 8, cols),
            shape(count // 4 + 2, 8, 128),
            shape(count // 4 + 2, 8, 128),
            shape(2, 8, 128),
        ),
        in_specs=[vm, vm],
        out_specs=[vm] * 4,
        scratch_shapes=[pltpu.VMEM((depth * rows, 128), F32)],
        compiler_params=params,
        name="pack",
    )(volume.reshape(depth * rows, cols), tissue_mask)

    def ring(x, axis, by):
        size = lax.axis_size(axis)
        return lax.ppermute(x, axis, [(i, (i + by) % size) for i in range(size)])

    def line(x, axis, by):
        size = lax.axis_size(axis)
        return lax.ppermute(x, axis, [(i, i + by) for i in range(size) if 0 <= i + by < size])

    def beyond(x, axis):
        return [ring(x, axis, by) for by in range(2, lax.axis_size(axis) - 1)]

    def swap(x):
        return lax.ppermute(x, "gx", [(c, c ^ 1) for c in range(lax.axis_size("gx"))])

    right = ring(low, "gx", -1)
    left = ring(high, "gx", 1)
    far = [] if lax.axis_size("gx") == 4 else beyond(sums, "gx")
    ordered = pl.pallas_call(
        order_kernel,
        out_shape=shape(count, 8, lanes),
        in_specs=[vm],
        out_specs=vm,
        compiler_params=params,
        cost_estimate=pl.CostEstimate(flops=5_000_000, bytes_accessed=1_000_000, transcendentals=0),
        name="order",
    )(own)
    half = pl.pallas_call(
        half_kernel,
        out_shape=shape(2, 8, 128),
        in_specs=[vm] * (3 + len(far)),
        out_specs=vm,
        compiler_params=params,
        name="half",
    )(left, right, sums, *far)
    other = swap(half)
    wide, top, bottom = pl.pallas_call(
        widen_kernel,
        out_shape=(
            shape(count, 8, lanes),
            shape(HALO + 1, 8, lanes),
            shape(HALO + 1, 8, lanes),
        ),
        in_specs=[vm] * 3,
        out_specs=[vm] * 3,
        input_output_aliases={0: 0},
        compiler_params=params,
        name="widen",
    )(ordered, left, right)
    below = line(top, "gy", -1)
    above = line(bottom, "gy", 1)
    state = [
        shape(5, full, 8, lanes),
        shape(3, full, 8, lanes),
        shape(len(FIELDS), full, 8, lanes),
        shape(4, spans, 8, lanes),
        shape(len(FIELDS), spans, 8, lanes),
    ]
    held = pl.pallas_call(
        inner_kernel,
        out_shape=state,
        in_specs=[vm],
        out_specs=[vm] * 5,
        compiler_params=params,
        cost_estimate=pl.CostEstimate(flops=20_000_000, bytes_accessed=8_000_000, transcendentals=0),
        name="inner",
    )(wide)
    other, *held = lax.optimization_barrier((other, *held))
    sums = pl.pallas_call(
        add_kernel,
        out_shape=shape(2, 8, 128),
        in_specs=[vm] * 2,
        out_specs=vm,
        compiler_params=params,
        name="add",
    )(half, other)
    far = [ring(sums, "gy", by) for by in range(1, lax.axis_size("gy"))]
    held = pl.pallas_call(
        outer_kernel,
        out_shape=state,
        in_specs=[vm] * 7,
        out_specs=[vm] * 5,
        input_output_aliases={2 + i: i for i in range(5)},
        compiler_params=params,
        cost_estimate=pl.CostEstimate(flops=20_000_000, bytes_accessed=8_000_000, transcendentals=0),
        name="outer",
    )(above, below, *held)
    out = pl.pallas_call(
        functools.partial(smooth_kernel, len(far)),
        out_shape=[shape(depth * rows, cols)] + state,
        in_specs=[vm] + [pl.BlockSpec(memory_space=pltpu.SMEM)] + [vm] * (len(far) + 5),
        out_specs=[vm] * 6,
        input_output_aliases={2 + len(far) + i: 1 + i for i in range(5)},
        scratch_shapes=[pltpu.VMEM((cols // 128, depth * rows, 128), F32)],
        compiler_params=params,
        name="smooth",
    )(sums, smoothing, *far, *held)[0]
    return out.reshape(depth, rows, cols)


def solution(mesh):
    placed = (P(None, ("slab", "gy"), "gx"), P(None, ("slab", "gy"), "gx"), P())
    return jax.shard_map(
        on_device,
        mesh=mesh,
        in_specs=placed,
        out_specs=P(None, ("slab", "gy"), "gx"),
        check_vma=False,
    )
```

```python
import functools

import jax
import jax.numpy as jnp
from jax import lax
from jax.experimental import pallas as pl
from jax.experimental.pallas import tpu as pltpu
from jax.sharding import PartitionSpec as P

F32 = jnp.float32
HALO = 18
OUT = HALO // 2
VMEM = pltpu.VMEM


def iotas():
    return (
        lax.broadcasted_iota(jnp.int32, (8, 128), 0),
        lax.broadcasted_iota(jnp.int32, (8, 128), 1),
    )


def lane_roll(x, by):
    return pltpu.roll(x, by % 128, 1)


def depth_roll(x, by):
    return pltpu.roll(x, by % 8, 0)


def picked(x, index):
    return jnp.take_along_axis(x, index, axis=1, mode="promise_in_bounds")


class Ring:
    def __init__(self, tiles):
        self.tiles = tiles
        lane = iotas()[1]
        self.lane = lane
        column = [lane * tiles + t for t in range(tiles)]
        self.index = [lax.rem(c, 128) for c in column]
        self.home = [lax.div(c, 128) for c in column]

    def own(self, x):
        result = []
        for index, home in zip(self.index, self.home):
            total = picked(x[0], index)
            for i in range(1, len(x)):
                total = jnp.where(home == i, picked(x[i], index), total)
            result.append(total)
        return result

    def edges(self, x, edge):
        last = self.tiles - 1
        return [
            jnp.where(home == last, picked(edge, index), v)
            for v, index, home in zip(x, self.index, self.home)
        ]

    def unpacked(self, left, right, group):
        edge = jnp.where(self.lane < HALO, lane_roll(right, -32 * group), 0.0)
        return jnp.where(self.lane >= 128 - HALO, lane_roll(left, 32 * (3 - group)), edge)

    def plain(self, x, count):
        result = []
        for t in range(count):
            column = self.lane + 128 * t
            index, home = lax.div(column, self.tiles), lax.rem(column, self.tiles)
            total = picked(x[0], index)
            for i in range(1, self.tiles):
                total = jnp.where(home == i, picked(x[i], index), total)
            result.append(total)
        return result


def split(ref, row, tiles):
    return [ref[row, :, t * 128 : (t + 1) * 128] for t in range(tiles)]


def put(ref, row, x):
    for t, v in enumerate(x):
        ref[row, :, t * 128 : (t + 1) * 128] = v


def odd_place():
    return lax.rem(lax.axis_index("gx"), 2)


def sides(core, chip):
    even = odd_place() == 0
    return jnp.where(even, chip, core), jnp.where(even, core, chip)


def pack_kernel(vol_ref, mask_ref, own_ref, core_ref, chip_ref, sums_ref, stage):
    even = odd_place() == 0
    cols = own_ref.shape[2]
    rows = own_ref.shape[0] - mask_ref.shape[1]
    blocks = mask_ref.shape[1]
    tiles = cols // 128
    sub, lane = iotas()
    wide = lax.broadcasted_iota(jnp.int32, (mask_ref.shape[2], cols), 1) // 8
    spread = (wide == lax.broadcasted_iota(jnp.int32, wide.shape, 0)).astype(F32)
    half = lax.broadcasted_iota(jnp.int32, (8, mask_ref.shape[2]), 0) < 4
    tissue = []
    for b in range(blocks):
        picked = jnp.where(half, mask_ref[0, b : b + 1, :], mask_ref[1, b : b + 1, :])
        t = jnp.dot(picked.astype(F32), spread, preferred_element_type=F32)
        own_ref[rows + b] = t
        tissue.append(t)
    total = jnp.zeros((8, 128), F32)
    count = jnp.zeros((8, 128), F32)
    for t in range(tiles):
        sl = slice(t * 128, (t + 1) * 128)
        stage[...] = vol_ref[:, sl]
        for b in range(blocks):
            part = jnp.zeros((8, 128), F32)
            for y in range(b * 8, b * 8 + 8):
                v = stage[pl.ds(y, 8, stride=rows), :]
                own_ref[y, :, sl] = v
                res = v - 0.5 * (depth_roll(v, 1) + depth_roll(v, -1))
                part = part + res * res
            total = total + part * tissue[b][:, sl]
            count = count + tissue[b][:, sl]
    inner = (sub >= 1) & (sub <= 6)
    total = jnp.where(inner, total * (2.0 / 3.0), 0.0)
    count = jnp.where(inner, count * 8.0, 0.0)
    sums_ref[0] = total
    sums_ref[1] = count
    packs = (rows + blocks) // 4
    group = lane // 32
    for k in range(packs):
        low = own_ref[4 * k, :, 0:128]
        high = lane_roll(own_ref[4 * k, :, cols - 128 : cols], 32)
        for g in range(1, 4):
            low = jnp.where(group == g, lane_roll(own_ref[4 * k + g, :, 0:128], 32 * g), low)
            high = jnp.where(
                group == g, lane_roll(own_ref[4 * k + g, :, cols - 128 : cols], 32 * (g + 1)), high
            )
        core_ref[k] = jnp.where(even, high, low)
        chip_ref[k] = jnp.where(even, low, high)
    for ref in (core_ref, chip_ref):
        ref[packs] = total
        ref[packs + 1] = count


def half_kernel(core_ref, chip_ref, own_ref, *refs):
    packs = core_ref.shape[0] - 2
    for i in range(2):
        beyond = own_ref[i] + chip_ref[packs + i]
        if len(refs) == 1:
            refs[-1][i] = beyond
        else:
            refs[-1][i] = 0.5 * functools.reduce(
                jnp.add, [ref[i] for ref in refs[:-1]], beyond + core_ref[packs + i]
            )


def add_kernel(a_ref, b_ref, out_ref):
    out_ref[...] = a_ref[...] + b_ref[...]


def order_kernel(own_ref, wide_ref):
    tiles = own_ref.shape[2] // 128
    ring = Ring(tiles + 1)
    for i in range(own_ref.shape[0]):
        put(wide_ref, i, ring.own(split(own_ref, i, tiles)))


def widen_kernel(part_ref, core_ref, chip_ref, wide_ref, top_ref, bottom_ref):
    tiles = wide_ref.shape[2] // 128
    count = wide_ref.shape[0]
    rows = count - count // 9
    ring = Ring(tiles)
    place = lax.axis_index("gx")
    has_left = (place > 0).astype(F32)
    has_right = (place < lax.axis_size("gx") - 1).astype(F32)
    for k in range(count // 4):
        left, right = sides(core_ref[k], chip_ref[k])
        left, right = left * has_left, right * has_right
        for g in range(4):
            i = 4 * k + g
            put(wide_ref, i, ring.edges(split(part_ref, i, tiles), ring.unpacked(left, right, g)))
    sub = iotas()[0]
    for ref, row, block in ((top_ref, 0, rows), (bottom_ref, rows - HALO, count - 3)):
        ref[0:HALO] = wide_ref[row : row + HALO]
        packed = [jnp.zeros((8, 128), F32)] * tiles
        for b in range(3):
            for i in range(2):
                some = [v[4 * i : 4 * i + 1] for v in split(wide_ref, block + b, tiles)]
                packed = [jnp.where(sub == 2 * b + i, x, y) for x, y in zip(some, packed)]
        put(ref, HALO, packed)


FIELDS = [(0, 8), (1, -8), (1, 0), (1, 8), (2, 8), (2, 0), (3, -8), (3, 0), (3, 8)]
APART = [f for f, (_, step) in enumerate(FIELDS) if step]
LEVEL = [f for f, (_, step) in enumerate(FIELDS) if not step]


class Steps:
    def __init__(self, val, cor, dist, tis, pair):
        self.val, self.cor, self.dist, self.tis, self.pair = val, cor, dist, tis, pair
        self.tiles = val.shape[-1] // 128
        self.tile = [slice(t * 128, (t + 1) * 128) for t in range(self.tiles)]
        self.sub, self.lane = iotas()
        self.edge34 = (self.sub == 3) | (self.sub == 4)
        self.edge04 = (self.sub == 0) | (self.sub == 4)
        self.edge37 = (self.sub == 3) | (self.sub == 7)

    def load(self, ref, *idx):
        return [ref[(*idx, slice(None), s)] for s in self.tile]

    def store(self, ref, x, *idx):
        for t, s in enumerate(self.tile):
            ref[(*idx, slice(None), s)] = x[t]

    def along(self, x, by):
        moved = []
        for j in range(self.tiles):
            lanes, source = divmod(j + by, self.tiles)
            moved.append(lane_roll(x[source], -lanes) if lanes else x[source])
        return moved

    def box_lanes(self, x):
        down, up = self.along(x, -1), self.along(x, 1)
        first = x[0] + up[0]
        second = first + up[1]
        return [first + down[0], second] + [
            (x[t] + down[t]) + up[t] for t in range(2, self.tiles)
        ]

    def box_rows(self, e):
        result = []
        for i in range(0, len(e) - 2, 2):
            middle = [a + b for a, b in zip(e[i + 1], e[i + 2])]
            result.append([a + b for a, b in zip(e[i], middle)])
            if i + 3 < len(e):
                result.append([a + b for a, b in zip(middle, e[i + 3])])
        return result

    def run(self, starts, number, group, fn):
        whole = number // group
        if whole:
            @pl.loop(0, whole)
            def _(i):
                for start in starts:
                    fn(start + i * group, group)
        if number % group:
            for start in starts:
                fn(start + whole * group, number % group)

    def tissue(self, spans):
        for b in spans:
            t0 = self.load(self.tis, 0, b)
            t1 = self.along(t0, 8)
            self.store(self.tis, t1, 1, b)
            self.store(self.tis, [depth_roll(v, 4) for v in t0], 2, b)
            self.store(self.tis, [depth_roll(v, 4) for v in t1], 3, b)

    def pairs(self, spans, level_spans):
        for f, (kind, step) in enumerate(FIELDS):
            for b in spans if step else level_spans:
                low, high = b, b + (1 if step else 0)
                p, q = (high, low) if step < 0 else (low, high)
                for s in self.tile:
                    self.pair[f, b, :, s] = self.tis[0, p, :, s] * self.tis[kind, q, :, s]

    def prepare(self, source):
        def fn(r, group):
            for i in range(group):
                v = self.load(self.val, source, r + i)
                v8 = self.along(v, 8)
                if source:
                    self.store(self.val, v, 0, r + i)
                self.store(self.val, v8, 1, r + i)
                self.store(self.val, [depth_roll(x, 4) for x in v], 2, r + i)
                self.store(self.val, [depth_roll(x, 4) for x in v8], 3, r + i)

        return fn

    def corrections(self, r, group):
        square = []
        for i in range(-1, group + 1):
            square.append([x * x for x in self.load(self.val, 0, r + i)])
        sums = self.box_rows(square)
        for base in range(0, group, 4):
            some = sums[base : base + 4]
            packed = [depth_roll(x, 4) for x in some[0]]
            for i, row in enumerate(some):
                for place, by in ((2 * i, 2 * i - 4), (2 * i + 1, 2 * i - 2)):
                    if place:
                        here = self.sub == place
                        packed = [
                            jnp.where(here, depth_roll(x, by), y) for x, y in zip(row, packed)
                        ]
            packed = self.box_lanes(packed)
            moved = self.along(packed, 8)
            for i in range(len(some)):
                y = r + base + i
                self.store(self.cor, [depth_roll(x, 3 - 2 * i) for x in packed], 0, y)
                self.store(self.cor, [depth_roll(x, 7 - 2 * i) for x in packed], 1, y)
                self.store(self.cor, [depth_roll(x, 7 - 2 * i) for x in moved], 2, y)

    def distances(self, fields):
        def fn(r, group):
            shared = {}
            for f in fields:
                kind, step = FIELDS[f]
                p = r + 8 if step < 0 else r
                q = r + 8 if step > 0 else r
                if (step < 0) not in shared:
                    shared[step < 0] = [
                        self.load(self.val, 0, p + i) for i in range(-1, group + 1)
                    ]
                e = []
                for i in range(-1, group + 1):
                    other = self.load(self.val, kind, q + i)
                    d = [a - b for a, b in zip(shared[step < 0][i + 1], other)]
                    e.append([x * x for x in d])
                for i, s in enumerate(self.box_rows(e)):
                    s = self.box_lanes(s)
                    up = [depth_roll(x, 1) for x in s]
                    down = [depth_roll(x, -1) for x in s]
                    if kind >= 2:
                        near = self.load(self.cor, 0, p + i)
                        far = self.load(self.cor, kind - 1, q + i)
                        c = [jnp.where(self.edge34, a, b) for a, b in zip(near, far)]
                        up = [jnp.where(self.edge04, a, b) for a, b in zip(c, up)]
                        down = [jnp.where(self.edge37, a, b) for a, b in zip(c, down)]
                    else:
                        up = [jnp.where(self.sub == 0, 0.0, b) for b in up]
                        down = [jnp.where(self.sub == 7, 0.0, b) for b in down]
                    self.store(
                        self.dist, [a + b + c for a, b, c in zip(s, up, down)], f, r + i
                    )

        return fn

    def weight(self, f, r, factor):
        both = self.load(self.pair, f, (r + 24 - HALO) // 8)
        d = self.load(self.dist, f, r)
        return [jnp.exp2(a * factor) * b for a, b in zip(d, both)]

    def early(self, factor):
        def fn(r, group):
            for i in range(group):
                for f in APART:
                    self.store(self.dist, self.weight(f, r + i, factor), f, r + i)

        return fn

    def combine(self, factor, put):
        def fn(r, group):
            for i in range(group):
                y = r + i
                centre = self.load(self.val, 0, y)
                own = self.load(self.tis, 0, (y + 24 - HALO) // 8)
                den = [None] * 4
                num = [None] * 4

                def add(frame, w, v):
                    if den[frame] is None:
                        den[frame] = list(w)
                        num[frame] = [a * b for a, b in zip(w, v)]
                    else:
                        den[frame] = [a + b for a, b in zip(den[frame], w)]
                        num[frame] = [n + a * b for n, a, b in zip(num[frame], w, v)]

                for f, (kind, step) in enumerate(FIELDS):
                    w = self.weight(f, y, factor)
                    before = w
                    if step:
                        before = self.load(self.dist, f, y - 8)
                        self.store(self.dist, w, f, y)
                    at_p, at_q = (before, w) if step < 0 else (w, before)
                    add(0, at_p, self.load(self.val, kind, y + step))
                    if (kind, step) != (2, 0):
                        add(kind, at_q, self.load(self.val, 0, y - step))
                result = []
                for acc in (den, num):
                    side = [a + depth_roll(b, 4) for a, b in zip(acc[1], acc[3])]
                    side = self.along(side, -8)
                    result.append(
                        [a + depth_roll(b, 4) + c for a, b, c in zip(acc[0], acc[2], side)]
                    )
                new = []
                for t in range(self.tiles):
                    n, d = result[1][t] + centre[t], result[0][t] + 1.0
                    new.append(jnp.where(own[t] > 0.0, n / d, centre[t]))
                put(y, new)

        return fn


def inner_kernel(wide_ref, val, cor, dist, tis, pair):
    count = wide_ref.shape[0]
    blocks = count // 9
    rows = count - blocks
    low, high = HALO, HALO + rows
    steps = Steps(val, cor, dist, tis, pair)
    val[0, low:high] = wide_ref[0:rows]
    tis[0, 3 : 3 + blocks] = wide_ref[rows:count]
    steps.tissue(range(3, 3 + blocks))
    steps.pairs(range(3, 2 + blocks), range(3, 3 + blocks))
    steps.run([low], rows, 16, steps.prepare(0))
    steps.run([low + 1], rows - 2, 15, steps.corrections)
    steps.run([low + 1], rows - 10, 11, steps.distances(APART))
    steps.run([low + 1], rows - 2, 10, steps.distances(LEVEL))


def outer_kernel(above_ref, below_ref, *refs):
    val, cor, dist, tis, pair = refs[5:]
    full = val.shape[1]
    rows = full - 2 * HALO
    spans = tis.shape[1]
    low, high = HALO, HALO + rows
    steps = Steps(val, cor, dist, tis, pair)

    for ref, row, block in ((above_ref, 0, 0), (below_ref, high, spans - 3)):
        val[0, row : row + HALO] = ref[0:HALO]
        packed = split(ref, HALO, steps.tiles)
        for b in range(3):
            steps.store(
                tis,
                [
                    jnp.where(steps.sub < 4, v[2 * b : 2 * b + 1], v[2 * b + 1 : 2 * b + 2])
                    for v in packed
                ],
                0,
                block + b,
            )
    ends = [*range(0, 3), *range(spans - 3, spans)]
    steps.tissue(ends)
    steps.pairs([*range(0, 3), *range(spans - 4, spans - 1)], ends)
    steps.run([0, high], HALO, 18, steps.prepare(0))
    steps.run([1, high - 1], HALO, 18, steps.corrections)
    steps.run([OUT - 8, high - 9], low + 1 - (OUT - 8), 9, steps.distances(APART))
    steps.run([OUT, high - 1], low + 1 - OUT, 10, steps.distances(LEVEL))


def smooth_kernel(fars, sums_ref, smoothing_ref, *refs):
    far_refs, refs = refs[:fars], refs[fars + 5 :]
    out_ref, val, cor, dist, tis, pair, stage = refs
    cols = out_ref.shape[1]
    full = val.shape[1]
    rows = full - 2 * HALO
    low = HALO
    steps = Steps(val, cor, dist, tis, pair)
    ring = Ring(steps.tiles)

    total, number = [
        jnp.sum(
            jnp.sum(
                functools.reduce(jnp.add, [ref[i] for ref in (sums_ref, *far_refs)]),
                axis=1,
                keepdims=True,
            ),
            axis=0,
            keepdims=True,
        )
        for i in range(2)
    ]
    variance = total / jnp.maximum(number, 1.0) + 1e-05
    h = smoothing_ref[0]
    inverse = 1.0 / (54.0 * h * h * variance)
    factor = jnp.broadcast_to(inverse * (-1.4426950408889634), (8, 128))

    def keep(y, new):
        steps.store(val, new, 4, y)

    def finish(y, new):
        for t, x in enumerate(ring.plain(new, cols // 128)):
            stage[t, pl.ds(y - HALO, 8, stride=rows), :] = x

    steps.run([OUT - 8], 8, 8, steps.early(factor))
    steps.run([OUT], full - 2 * OUT, 5, steps.combine(factor, keep))

    steps.run([OUT], full - 2 * OUT, 25, steps.prepare(4))
    steps.run([OUT + 1], full - 2 * OUT - 2, 16, steps.corrections)
    steps.run([low - 8], rows + 8, 10, steps.distances(APART))
    steps.run([low], rows, 8, steps.distances(LEVEL))
    steps.run([low - 8], 8, 8, steps.early(factor))
    steps.run([low], rows, 8, steps.combine(factor, finish))
    for t in range(cols // 128):
        out_ref[:, t * 128 : (t + 1) * 128] = stage[t]


def on_device(volume, tissue_mask, smoothing):
    depth, rows, cols = volume.shape
    blocks = tissue_mask.shape[1]
    count = rows + blocks
    lanes = cols + 128
    full = rows + 2 * HALO
    spans = blocks + 6
    vm = pl.BlockSpec(memory_space=VMEM)
    shape = lambda *s: jax.ShapeDtypeStruct(s, F32)
    params = pltpu.CompilerParams(vmem_limit_bytes=32 * 1024 * 1024)
    own, core, chip, sums = pl.pallas_call(
        pack_kernel,
        out_shape=(
            shape(count, 8, cols),
            shape(count // 4 + 2, 8, 128),
            shape(count // 4 + 2, 8, 128),
            shape(2, 8, 128),
        ),
        in_specs=[vm, vm],
        out_specs=[vm] * 4,
        scratch_shapes=[pltpu.VMEM((depth * rows, 128), F32)],
        compiler_params=params,
        name="pack",
    )(volume.reshape(depth * rows, cols), tissue_mask)

    def ring(x, axis, by):
        size = lax.axis_size(axis)
        return lax.ppermute(x, axis, [(i, (i + by) % size) for i in range(size)])

    def line(x, axis, by):
        size = lax.axis_size(axis)
        return lax.ppermute(x, axis, [(i, i + by) for i in range(size) if 0 <= i + by < size])

    def beyond(x, axis):
        return [ring(x, axis, by) for by in range(2, lax.axis_size(axis) - 1)]

    def swap(x):
        return lax.ppermute(x, "gx", [(c, c ^ 1) for c in range(lax.axis_size("gx"))])

    size = lax.axis_size("gx")
    chip = lax.ppermute(chip, "gx", [(i, (i + (1 if i % 2 else -1)) % size) for i in range(size)])
    core = swap(core)
    far = [] if lax.axis_size("gx") == 4 else beyond(sums, "gx")
    ordered = pl.pallas_call(
        order_kernel,
        out_shape=shape(count, 8, lanes),
        in_specs=[vm],
        out_specs=vm,
        compiler_params=params,
        cost_estimate=pl.CostEstimate(flops=5_000_000, bytes_accessed=1_000_000, transcendentals=0),
        name="order",
    )(own)
    half = pl.pallas_call(
        half_kernel,
        out_shape=shape(2, 8, 128),
        in_specs=[vm] * (3 + len(far)),
        out_specs=vm,
        compiler_params=params,
        name="half",
    )(core, chip, sums, *far)
    other = swap(half)
    wide, top, bottom = pl.pallas_call(
        widen_kernel,
        out_shape=(
            shape(count, 8, lanes),
            shape(HALO + 1, 8, lanes),
            shape(HALO + 1, 8, lanes),
        ),
        in_specs=[vm] * 3,
        out_specs=[vm] * 3,
        input_output_aliases={0: 0},
        compiler_params=params,
        name="widen",
    )(ordered, core, chip)
    below = line(top, "gy", -1)
    above = line(bottom, "gy", 1)
    state = [
        shape(5, full, 8, lanes),
        shape(3, full, 8, lanes),
        shape(len(FIELDS), full, 8, lanes),
        shape(4, spans, 8, lanes),
        shape(len(FIELDS), spans, 8, lanes),
    ]
    held = pl.pallas_call(
        inner_kernel,
        out_shape=state,
        in_specs=[vm],
        out_specs=[vm] * 5,
        compiler_params=params,
        cost_estimate=pl.CostEstimate(flops=20_000_000, bytes_accessed=8_000_000, transcendentals=0),
        name="inner",
    )(wide)
    other, *held = lax.optimization_barrier((other, *held))
    sums = pl.pallas_call(
        add_kernel,
        out_shape=shape(2, 8, 128),
        in_specs=[vm] * 2,
        out_specs=vm,
        compiler_params=params,
        name="add",
    )(half, other)
    far = [ring(sums, "gy", by) for by in range(1, lax.axis_size("gy"))]
    held = pl.pallas_call(
        outer_kernel,
        out_shape=state,
        in_specs=[vm] * 7,
        out_specs=[vm] * 5,
        input_output_aliases={2 + i: i for i in range(5)},
        compiler_params=params,
        cost_estimate=pl.CostEstimate(flops=20_000_000, bytes_accessed=8_000_000, transcendentals=0),
        name="outer",
    )(above, below, *held)
    out = pl.pallas_call(
        functools.partial(smooth_kernel, len(far)),
        out_shape=[shape(depth * rows, cols)] + state,
        in_specs=[vm] + [pl.BlockSpec(memory_space=pltpu.SMEM)] + [vm] * (len(far) + 5),
        out_specs=[vm] * 6,
        input_output_aliases={2 + len(far) + i: 1 + i for i in range(5)},
        scratch_shapes=[pltpu.VMEM((cols // 128, depth * rows, 128), F32)],
        compiler_params=params,
        name="smooth",
    )(sums, smoothing, *far, *held)[0]
    return out.reshape(depth, rows, cols)


def solution(mesh):
    placed = (P(None, ("slab", "gy"), "gx"), P(None, ("slab", "gy"), "gx"), P())
    return jax.shard_map(
        on_device,
        mesh=mesh,
        in_specs=placed,
        out_specs=P(None, ("slab", "gy"), "gx"),
        check_vma=False,
    )
```

```python
import functools

import jax
import jax.numpy as jnp
from jax import lax
from jax.experimental import pallas as pl
from jax.experimental.pallas import tpu as pltpu
from jax.sharding import PartitionSpec as P

F32 = jnp.float32
HALO = 18
OUT = HALO // 2
VMEM = pltpu.VMEM


def iotas():
    return (
        lax.broadcasted_iota(jnp.int32, (8, 128), 0),
        lax.broadcasted_iota(jnp.int32, (8, 128), 1),
    )


def lane_roll(x, by):
    return pltpu.roll(x, by % 128, 1)


def depth_roll(x, by):
    return pltpu.roll(x, by % 8, 0)


def picked(x, index):
    return jnp.take_along_axis(x, index, axis=1, mode="promise_in_bounds")


class Ring:
    def __init__(self, tiles):
        self.tiles = tiles
        lane = iotas()[1]
        self.lane = lane
        column = [lane * tiles + t for t in range(tiles)]
        self.index = [lax.rem(c, 128) for c in column]
        self.home = [lax.div(c, 128) for c in column]

    def own(self, x):
        result = []
        for index, home in zip(self.index, self.home):
            total = picked(x[0], index)
            for i in range(1, len(x)):
                total = jnp.where(home == i, picked(x[i], index), total)
            result.append(total)
        return result

    def edges(self, x, edge):
        last = self.tiles - 1
        return [
            jnp.where(home == last, picked(edge, index), v)
            for v, index, home in zip(x, self.index, self.home)
        ]

    def unpacked(self, left, right, group):
        edge = jnp.where(self.lane < HALO, lane_roll(right, -32 * group), 0.0)
        return jnp.where(self.lane >= 128 - HALO, lane_roll(left, 32 * (3 - group)), edge)

    def plain(self, x, count):
        result = []
        for t in range(count):
            column = self.lane + 128 * t
            index, home = lax.div(column, self.tiles), lax.rem(column, self.tiles)
            total = picked(x[0], index)
            for i in range(1, self.tiles):
                total = jnp.where(home == i, picked(x[i], index), total)
            result.append(total)
        return result


def split(ref, row, tiles):
    return [ref[row, :, t * 128 : (t + 1) * 128] for t in range(tiles)]


def put(ref, row, x):
    for t, v in enumerate(x):
        ref[row, :, t * 128 : (t + 1) * 128] = v


def odd_place():
    return lax.rem(lax.axis_index("gx"), 2)


def sides(core, chip):
    even = odd_place() == 0
    return jnp.where(even, chip, core), jnp.where(even, core, chip)


def pack_kernel(vol_ref, mask_ref, own_ref, core_ref, chip_ref, sums_ref, stage):
    even = odd_place() == 0
    cols = own_ref.shape[2]
    rows = own_ref.shape[0] - mask_ref.shape[1]
    blocks = mask_ref.shape[1]
    tiles = cols // 128
    sub, lane = iotas()
    wide = lax.broadcasted_iota(jnp.int32, (mask_ref.shape[2], cols), 1) // 8
    spread = (wide == lax.broadcasted_iota(jnp.int32, wide.shape, 0)).astype(F32)
    half = lax.broadcasted_iota(jnp.int32, (8, mask_ref.shape[2]), 0) < 4
    tissue = []
    for b in range(blocks):
        picked = jnp.where(half, mask_ref[0, b : b + 1, :], mask_ref[1, b : b + 1, :])
        t = jnp.dot(picked.astype(F32), spread, preferred_element_type=F32)
        own_ref[rows + b] = t
        tissue.append(t)
    total = jnp.zeros((8, 128), F32)
    count = jnp.zeros((8, 128), F32)
    for t in range(tiles):
        sl = slice(t * 128, (t + 1) * 128)
        stage[...] = vol_ref[:, sl]
        for b in range(blocks):
            part = jnp.zeros((8, 128), F32)
            for y in range(b * 8, b * 8 + 8):
                v = stage[pl.ds(y, 8, stride=rows), :]
                own_ref[y, :, sl] = v
                res = v - 0.5 * (depth_roll(v, 1) + depth_roll(v, -1))
                part = part + res * res
            total = total + part * tissue[b][:, sl]
            count = count + tissue[b][:, sl]
    inner = (sub >= 1) & (sub <= 6)
    total = jnp.where(inner, total * (2.0 / 3.0), 0.0)
    count = jnp.where(inner, count * 8.0, 0.0)
    sums_ref[0] = total
    sums_ref[1] = count
    packs = (rows + blocks) // 4
    group = lane // 32
    for k in range(packs):
        low = own_ref[4 * k, :, 0:128]
        high = lane_roll(own_ref[4 * k, :, cols - 128 : cols], 32)
        for g in range(1, 4):
            low = jnp.where(group == g, lane_roll(own_ref[4 * k + g, :, 0:128], 32 * g), low)
            high = jnp.where(
                group == g, lane_roll(own_ref[4 * k + g, :, cols - 128 : cols], 32 * (g + 1)), high
            )
        core_ref[k] = jnp.where(even, high, low)
        chip_ref[k] = jnp.where(even, low, high)
    for ref in (core_ref, chip_ref):
        ref[packs] = total
        ref[packs + 1] = count


def half_kernel(core_ref, chip_ref, own_ref, *refs):
    packs = core_ref.shape[0] - 2
    for i in range(2):
        beyond = own_ref[i] + chip_ref[packs + i]
        if len(refs) == 1:
            refs[-1][i] = beyond
        else:
            refs[-1][i] = 0.5 * functools.reduce(
                jnp.add, [ref[i] for ref in refs[:-1]], beyond + core_ref[packs + i]
            )


def add_kernel(a_ref, b_ref, out_ref):
    out_ref[...] = a_ref[...] + b_ref[...]


def order_kernel(own_ref, wide_ref):
    tiles = own_ref.shape[2] // 128
    ring = Ring(tiles + 1)
    for i in range(own_ref.shape[0]):
        put(wide_ref, i, ring.own(split(own_ref, i, tiles)))


def widen_kernel(part_ref, core_ref, chip_ref, wide_ref, top_ref, bottom_ref):
    tiles = wide_ref.shape[2] // 128
    count = wide_ref.shape[0]
    rows = count - count // 9
    ring = Ring(tiles)
    place = lax.axis_index("gx")
    has_left = (place > 0).astype(F32)
    has_right = (place < lax.axis_size("gx") - 1).astype(F32)
    for k in range(count // 4):
        left, right = sides(core_ref[k], chip_ref[k])
        left, right = left * has_left, right * has_right
        for g in range(4):
            i = 4 * k + g
            put(wide_ref, i, ring.edges(split(part_ref, i, tiles), ring.unpacked(left, right, g)))
    sub = iotas()[0]
    for ref, row, block in ((top_ref, 0, rows), (bottom_ref, rows - HALO, count - 3)):
        ref[0:HALO] = wide_ref[row : row + HALO]
        packed = [jnp.zeros((8, 128), F32)] * tiles
        for b in range(3):
            for i in range(2):
                some = [v[4 * i : 4 * i + 1] for v in split(wide_ref, block + b, tiles)]
                packed = [jnp.where(sub == 2 * b + i, x, y) for x, y in zip(some, packed)]
        put(ref, HALO, packed)


FIELDS = [(0, 8), (1, -8), (1, 0), (1, 8), (2, 8), (2, 0), (3, -8), (3, 0), (3, 8)]
APART = [f for f, (_, step) in enumerate(FIELDS) if step]
LEVEL = [f for f, (_, step) in enumerate(FIELDS) if not step]


class Steps:
    def __init__(self, val, cor, dist, tis, pair):
        self.val, self.cor, self.dist, self.tis, self.pair = val, cor, dist, tis, pair
        self.tiles = val.shape[-1] // 128
        self.tile = [slice(t * 128, (t + 1) * 128) for t in range(self.tiles)]
        self.sub, self.lane = iotas()
        self.edge34 = (self.sub == 3) | (self.sub == 4)
        self.edge04 = (self.sub == 0) | (self.sub == 4)
        self.edge37 = (self.sub == 3) | (self.sub == 7)

    def load(self, ref, *idx):
        return [ref[(*idx, slice(None), s)] for s in self.tile]

    def store(self, ref, x, *idx):
        for t, s in enumerate(self.tile):
            ref[(*idx, slice(None), s)] = x[t]

    def along(self, x, by):
        moved = []
        for j in range(self.tiles):
            lanes, source = divmod(j + by, self.tiles)
            moved.append(lane_roll(x[source], -lanes) if lanes else x[source])
        return moved

    def box_lanes(self, x):
        down, up = self.along(x, -1), self.along(x, 1)
        first = x[0] + up[0]
        second = first + up[1]
        return [first + down[0], second] + [
            (x[t] + down[t]) + up[t] for t in range(2, self.tiles)
        ]

    def box_rows(self, e):
        result = []
        for i in range(0, len(e) - 2, 2):
            middle = [a + b for a, b in zip(e[i + 1], e[i + 2])]
            result.append([a + b for a, b in zip(e[i], middle)])
            if i + 3 < len(e):
                result.append([a + b for a, b in zip(middle, e[i + 3])])
        return result

    def run(self, starts, number, group, fn):
        whole = number // group
        if whole:
            @pl.loop(0, whole)
            def _(i):
                for start in starts:
                    fn(start + i * group, group)
        if number % group:
            for start in starts:
                fn(start + whole * group, number % group)

    def tissue(self, spans):
        for b in spans:
            t0 = self.load(self.tis, 0, b)
            t1 = self.along(t0, 8)
            self.store(self.tis, t1, 1, b)
            self.store(self.tis, [depth_roll(v, 4) for v in t0], 2, b)
            self.store(self.tis, [depth_roll(v, 4) for v in t1], 3, b)

    def pairs(self, spans, level_spans):
        for f, (kind, step) in enumerate(FIELDS):
            for b in spans if step else level_spans:
                low, high = b, b + (1 if step else 0)
                p, q = (high, low) if step < 0 else (low, high)
                for s in self.tile:
                    self.pair[f, b, :, s] = self.tis[0, p, :, s] * self.tis[kind, q, :, s]

    def prepare(self, source):
        def fn(r, group):
            for i in range(group):
                v = self.load(self.val, source, r + i)
                v8 = self.along(v, 8)
                if source:
                    self.store(self.val, v, 0, r + i)
                self.store(self.val, v8, 1, r + i)
                self.store(self.val, [depth_roll(x, 4) for x in v], 2, r + i)
                self.store(self.val, [depth_roll(x, 4) for x in v8], 3, r + i)

        return fn

    def corrections(self, r, group):
        square = []
        for i in range(-1, group + 1):
            square.append([x * x for x in self.load(self.val, 0, r + i)])
        sums = self.box_rows(square)
        for base in range(0, group, 4):
            some = sums[base : base + 4]
            packed = [depth_roll(x, 4) for x in some[0]]
            for i, row in enumerate(some):
                for place, by in ((2 * i, 2 * i - 4), (2 * i + 1, 2 * i - 2)):
                    if place:
                        here = self.sub == place
                        packed = [
                            jnp.where(here, depth_roll(x, by), y) for x, y in zip(row, packed)
                        ]
            packed = self.box_lanes(packed)
            moved = self.along(packed, 8)
            for i in range(len(some)):
                y = r + base + i
                self.store(self.cor, [depth_roll(x, 3 - 2 * i) for x in packed], 0, y)
                self.store(self.cor, [depth_roll(x, 7 - 2 * i) for x in packed], 1, y)
                self.store(self.cor, [depth_roll(x, 7 - 2 * i) for x in moved], 2, y)

    def distances(self, fields):
        def fn(r, group):
            shared = {}
            for f in fields:
                kind, step = FIELDS[f]
                p = r + 8 if step < 0 else r
                q = r + 8 if step > 0 else r
                if (step < 0) not in shared:
                    shared[step < 0] = [
                        self.load(self.val, 0, p + i) for i in range(-1, group + 1)
                    ]
                e = []
                for i in range(-1, group + 1):
                    other = self.load(self.val, kind, q + i)
                    d = [a - b for a, b in zip(shared[step < 0][i + 1], other)]
                    e.append([x * x for x in d])
                for i, s in enumerate(self.box_rows(e)):
                    s = self.box_lanes(s)
                    up = [depth_roll(x, 1) for x in s]
                    down = [depth_roll(x, -1) for x in s]
                    if kind >= 2:
                        near = self.load(self.cor, 0, p + i)
                        far = self.load(self.cor, kind - 1, q + i)
                        c = [jnp.where(self.edge34, a, b) for a, b in zip(near, far)]
                        up = [jnp.where(self.edge04, a, b) for a, b in zip(c, up)]
                        down = [jnp.where(self.edge37, a, b) for a, b in zip(c, down)]
                    else:
                        up = [jnp.where(self.sub == 0, 0.0, b) for b in up]
                        down = [jnp.where(self.sub == 7, 0.0, b) for b in down]
                    self.store(
                        self.dist, [a + b + c for a, b, c in zip(s, up, down)], f, r + i
                    )

        return fn

    def weight(self, f, r, factor):
        both = self.load(self.pair, f, (r + 24 - HALO) // 8)
        d = self.load(self.dist, f, r)
        return [jnp.exp2(a * factor) * b for a, b in zip(d, both)]

    def early(self, factor):
        def fn(r, group):
            for i in range(group):
                for f in APART:
                    self.store(self.dist, self.weight(f, r + i, factor), f, r + i)

        return fn

    def combine(self, factor, put):
        def fn(r, group):
            for i in range(group):
                y = r + i
                centre = self.load(self.val, 0, y)
                own = self.load(self.tis, 0, (y + 24 - HALO) // 8)
                den = [None] * 4
                num = [None] * 4

                def add(frame, w, v):
                    if den[frame] is None:
                        den[frame] = list(w)
                        num[frame] = [a * b for a, b in zip(w, v)]
                    else:
                        den[frame] = [a + b for a, b in zip(den[frame], w)]
                        num[frame] = [n + a * b for n, a, b in zip(num[frame], w, v)]

                for f, (kind, step) in enumerate(FIELDS):
                    w = self.weight(f, y, factor)
                    before = w
                    if step:
                        before = self.load(self.dist, f, y - 8)
                        self.store(self.dist, w, f, y)
                    at_p, at_q = (before, w) if step < 0 else (w, before)
                    add(0, at_p, self.load(self.val, kind, y + step))
                    if (kind, step) != (2, 0):
                        add(kind, at_q, self.load(self.val, 0, y - step))
                result = []
                for acc in (den, num):
                    side = [a + depth_roll(b, 4) for a, b in zip(acc[1], acc[3])]
                    side = self.along(side, -8)
                    result.append(
                        [a + depth_roll(b, 4) + c for a, b, c in zip(acc[0], acc[2], side)]
                    )
                new = []
                for t in range(self.tiles):
                    n, d = result[1][t] + centre[t], result[0][t] + 1.0
                    new.append(jnp.where(own[t] > 0.0, n / d, centre[t]))
                put(y, new)

        return fn


def inner_kernel(wide_ref, val, cor, dist, tis, pair):
    count = wide_ref.shape[0]
    blocks = count // 9
    rows = count - blocks
    low, high = HALO, HALO + rows
    steps = Steps(val, cor, dist, tis, pair)
    val[0, low:high] = wide_ref[0:rows]
    tis[0, 3 : 3 + blocks] = wide_ref[rows:count]
    steps.tissue(range(3, 3 + blocks))
    steps.pairs(range(3, 2 + blocks), range(3, 3 + blocks))
    steps.run([low], rows, 16, steps.prepare(0))
    steps.run([low + 1], rows - 2, 15, steps.corrections)
    steps.run([low + 1], rows - 10, 11, steps.distances(APART))
    steps.run([low + 1], rows - 2, 10, steps.distances(LEVEL))


def outer_kernel(above_ref, below_ref, *refs):
    val, cor, dist, tis, pair = refs[5:]
    full = val.shape[1]
    rows = full - 2 * HALO
    spans = tis.shape[1]
    low, high = HALO, HALO + rows
    steps = Steps(val, cor, dist, tis, pair)

    for ref, row, block in ((above_ref, 0, 0), (below_ref, high, spans - 3)):
        val[0, row : row + HALO] = ref[0:HALO]
        packed = split(ref, HALO, steps.tiles)
        for b in range(3):
            steps.store(
                tis,
                [
                    jnp.where(steps.sub < 4, v[2 * b : 2 * b + 1], v[2 * b + 1 : 2 * b + 2])
                    for v in packed
                ],
                0,
                block + b,
            )
    ends = [*range(0, 3), *range(spans - 3, spans)]
    steps.tissue(ends)
    steps.pairs([*range(0, 3), *range(spans - 4, spans - 1)], ends)
    steps.run([0, high], HALO, 18, steps.prepare(0))
    steps.run([1, high - 1], HALO, 18, steps.corrections)
    steps.run([OUT - 8, high - 9], low + 1 - (OUT - 8), 9, steps.distances(APART))
    steps.run([OUT, high - 1], low + 1 - OUT, 10, steps.distances(LEVEL))


def smooth_kernel(fars, sums_ref, smoothing_ref, *refs):
    far_refs, refs = refs[:fars], refs[fars + 5 :]
    out_ref, val, cor, dist, tis, pair, stage = refs
    cols = out_ref.shape[1]
    full = val.shape[1]
    rows = full - 2 * HALO
    low = HALO
    steps = Steps(val, cor, dist, tis, pair)
    ring = Ring(steps.tiles)

    total, number = [
        jnp.sum(
            jnp.sum(
                functools.reduce(jnp.add, [ref[i] for ref in (sums_ref, *far_refs)]),
                axis=1,
                keepdims=True,
            ),
            axis=0,
            keepdims=True,
        )
        for i in range(2)
    ]
    variance = total / jnp.maximum(number, 1.0) + 1e-05
    h = smoothing_ref[0]
    inverse = 1.0 / (54.0 * h * h * variance)
    factor = jnp.broadcast_to(inverse * (-1.4426950408889634), (8, 128))

    def keep(y, new):
        steps.store(val, new, 4, y)

    def finish(y, new):
        for t, x in enumerate(ring.plain(new, cols // 128)):
            stage[t, pl.ds(y - HALO, 8, stride=rows), :] = x

    steps.run([OUT - 8], 8, 8, steps.early(factor))
    steps.run([OUT], full - 2 * OUT, 5, steps.combine(factor, keep))

    steps.run([OUT], full - 2 * OUT, 25, steps.prepare(4))
    steps.run([OUT + 1], full - 2 * OUT - 2, 24, steps.corrections)
    steps.run([low - 8], rows + 8, 10, steps.distances(APART))
    steps.run([low], rows, 16, steps.distances(LEVEL))
    steps.run([low - 8], 8, 8, steps.early(factor))
    steps.run([low], rows, 8, steps.combine(factor, finish))
    for t in range(cols // 128):
        out_ref[:, t * 128 : (t + 1) * 128] = stage[t]


def on_device(volume, tissue_mask, smoothing):
    depth, rows, cols = volume.shape
    blocks = tissue_mask.shape[1]
    count = rows + blocks
    lanes = cols + 128
    full = rows + 2 * HALO
    spans = blocks + 6
    vm = pl.BlockSpec(memory_space=VMEM)
    shape = lambda *s: jax.ShapeDtypeStruct(s, F32)
    params = pltpu.CompilerParams(vmem_limit_bytes=32 * 1024 * 1024)
    own, core, chip, sums = pl.pallas_call(
        pack_kernel,
        out_shape=(
            shape(count, 8, cols),
            shape(count // 4 + 2, 8, 128),
            shape(count // 4 + 2, 8, 128),
            shape(2, 8, 128),
        ),
        in_specs=[vm, vm],
        out_specs=[vm] * 4,
        scratch_shapes=[pltpu.VMEM((depth * rows, 128), F32)],
        compiler_params=params,
        name="pack",
    )(volume.reshape(depth * rows, cols), tissue_mask)

    def ring(x, axis, by):
        size = lax.axis_size(axis)
        return lax.ppermute(x, axis, [(i, (i + by) % size) for i in range(size)])

    def line(x, axis, by):
        size = lax.axis_size(axis)
        return lax.ppermute(x, axis, [(i, i + by) for i in range(size) if 0 <= i + by < size])

    def beyond(x, axis):
        return [ring(x, axis, by) for by in range(2, lax.axis_size(axis) - 1)]

    def swap(x):
        return lax.ppermute(x, "gx", [(c, c ^ 1) for c in range(lax.axis_size("gx"))])

    size = lax.axis_size("gx")
    chip = lax.ppermute(chip, "gx", [(i, (i + (1 if i % 2 else -1)) % size) for i in range(size)])
    core = swap(core)
    far = [] if lax.axis_size("gx") == 4 else beyond(sums, "gx")
    ordered = pl.pallas_call(
        order_kernel,
        out_shape=shape(count, 8, lanes),
        in_specs=[vm],
        out_specs=vm,
        compiler_params=params,
        cost_estimate=pl.CostEstimate(flops=5_000_000, bytes_accessed=1_000_000, transcendentals=0),
        name="order",
    )(own)
    half = pl.pallas_call(
        half_kernel,
        out_shape=shape(2, 8, 128),
        in_specs=[vm] * (3 + len(far)),
        out_specs=vm,
        compiler_params=params,
        name="half",
    )(core, chip, sums, *far)
    other = swap(half)
    wide, top, bottom = pl.pallas_call(
        widen_kernel,
        out_shape=(
            shape(count, 8, lanes),
            shape(HALO + 1, 8, lanes),
            shape(HALO + 1, 8, lanes),
        ),
        in_specs=[vm] * 3,
        out_specs=[vm] * 3,
        input_output_aliases={0: 0},
        compiler_params=params,
        name="widen",
    )(ordered, core, chip)
    below = line(top, "gy", -1)
    above = line(bottom, "gy", 1)
    state = [
        shape(5, full, 8, lanes),
        shape(3, full, 8, lanes),
        shape(len(FIELDS), full, 8, lanes),
        shape(4, spans, 8, lanes),
        shape(len(FIELDS), spans, 8, lanes),
    ]
    held = pl.pallas_call(
        inner_kernel,
        out_shape=state,
        in_specs=[vm],
        out_specs=[vm] * 5,
        compiler_params=params,
        cost_estimate=pl.CostEstimate(flops=20_000_000, bytes_accessed=8_000_000, transcendentals=0),
        name="inner",
    )(wide)
    other, *held = lax.optimization_barrier((other, *held))
    sums = pl.pallas_call(
        add_kernel,
        out_shape=shape(2, 8, 128),
        in_specs=[vm] * 2,
        out_specs=vm,
        compiler_params=params,
        name="add",
    )(half, other)
    far = [ring(sums, "gy", by) for by in range(1, lax.axis_size("gy"))]
    held = pl.pallas_call(
        outer_kernel,
        out_shape=state,
        in_specs=[vm] * 7,
        out_specs=[vm] * 5,
        input_output_aliases={2 + i: i for i in range(5)},
        compiler_params=params,
        cost_estimate=pl.CostEstimate(flops=20_000_000, bytes_accessed=8_000_000, transcendentals=0),
        name="outer",
    )(above, below, *held)
    out = pl.pallas_call(
        functools.partial(smooth_kernel, len(far)),
        out_shape=[shape(depth * rows, cols)] + state,
        in_specs=[vm] + [pl.BlockSpec(memory_space=pltpu.SMEM)] + [vm] * (len(far) + 5),
        out_specs=[vm] * 6,
        input_output_aliases={2 + len(far) + i: 1 + i for i in range(5)},
        scratch_shapes=[pltpu.VMEM((cols // 128, depth * rows, 128), F32)],
        compiler_params=params,
        name="smooth",
    )(sums, smoothing, *far, *held)[0]
    return out.reshape(depth, rows, cols)


def solution(mesh):
    placed = (P(None, ("slab", "gy"), "gx"), P(None, ("slab", "gy"), "gx"), P())
    return jax.shard_map(
        on_device,
        mesh=mesh,
        in_specs=placed,
        out_specs=P(None, ("slab", "gy"), "gx"),
        check_vma=False,
    )
```
